128 devices in a mesh: dp: 8 (over z, core), expert: 16 (over x, y).
Axes of the slice: x: 4, y: 4, z: 4, core: 2. Of those that a mesh axis runs over, the one named last changes fastest.
Arguments:
- tokens_in: bfloat16 [16384, 4096], P(('dp', 'expert')), may hold values from -6 to 6
- out_grad: bfloat16 [16384, 4096], P(('dp', 'expert')), may hold values from -6 to 6
- expert_ids: int32 [16384, 2], P(('dp', 'expert')), may hold values from 0 to 15, as said below
- router_codes: int32 [16384, 2], P(('dp', 'expert')), may hold values from 1 to 64
- amax_history: int32 [16, 4], replicated, may hold values from -2 to 2
- w_gate: bfloat16 [16, 4096, 768], P('expert'), may hold values from -0.09375 to 0.09375
- w_up: bfloat16 [16, 4096, 768], P('expert'), may hold values from -0.09375 to 0.09375
- w_down: bfloat16 [16, 768, 4096], P('expert'), may hold values from -0.21875 to 0.21875
Outputs:
- grad_tokens: bfloat16 [16384, 4096], P(('dp', 'expert'))
- grad_gate: bfloat16 [16, 4096, 768], P('expert', 'dp')
- grad_up: bfloat16 [16, 4096, 768], P('expert', 'dp')
- grad_down: bfloat16 [16, 768, 4096], P('expert', None, 'dp')
The draws below stay inside these ranges and needn't reach their ends.
Inputs may be any that keep to these rules, and one draw needn't show every extreme that they name: `expert_ids`: each row names 2 different experts. Among the 128 rows of one device no expert is named more than 32 times; in each data group one expert is named exactly 32 times by every device of the group.
All inputs are finite; a program needn't handle non-finite values.
Results may differ from the reference program's by a relative error of at most 0.017.
Values may be sent and summed in bfloat16 or wider, within the bound.
No kernel may reach another device: no remote copies, remote signals or barrier semaphores. Data moves between devices by JAX's collectives and lax.ppermute only.
A program may use at most 128 MiB of HBM per device.

```python
import jax
import jax.numpy as jnp
from jax import lax

D = 4096
H = 768
TOPK = 2
HIST = 4
TOK_DEV = 128
EXPERTS = 16
TOKENS = 16384
CAP = 32
N_DP = 8


def draw_expert_ids(key, part):
    key = jax.random.fold_in(key, 11)
    devices = TOKENS // TOK_DEV
    groups = devices // EXPERTS
    pairs = TOK_DEV * TOPK
    remaining = pairs - CAP
    hottest = jax.random.randint(jax.random.fold_in(key, 1), (groups,), 0, EXPERTS)

    def one_device(device):
        local = jax.random.fold_in(key, device + 2)
        first_key, second_key, third_key = jax.random.split(local, 3)
        chosen = hottest[device // EXPERTS]
        others = jax.random.permutation(first_key, EXPERTS - 1).astype(jnp.int32)
        others = others + (others >= chosen).astype(jnp.int32)
        tickets = jax.random.permutation(second_key, (EXPERTS - 1) * CAP)[:remaining] // CAP
        counts_other = jnp.sum((tickets[:, None] == jnp.arange(EXPERTS - 1)[None, :]).astype(jnp.int32), axis=0)
        order = jnp.concatenate([chosen[None].astype(jnp.int32), others])
        counts = jnp.concatenate([jnp.full((1,), CAP, jnp.int32), counts_other.astype(jnp.int32)])
        ends = jnp.cumsum(counts)
        positions = jnp.arange(pairs, dtype=jnp.int32)
        where_run = jnp.sum((positions[:, None] >= ends[None, :]).astype(jnp.int32), axis=1)
        sequence = order[where_run]
        ids = sequence.reshape(TOPK, TOK_DEV).T
        shuffle = jax.random.permutation(third_key, TOK_DEV)
        return ids[shuffle]
    drawn = jax.vmap(one_device)(jnp.arange(devices, dtype=jnp.int32))
    return drawn.reshape(TOKENS, TOPK).astype(jnp.int32)


def set_ends(entries, rng, low, largest):
    index_at = [jax.random.randint(jax.random.fold_in(rng, axis), (), 0, length) for axis, length in enumerate(entries.shape)]
    main_axis = entries.shape.index(max(entries.shape))
    neighbour = index_at[:main_axis] + [(index_at[main_axis] + 1) % entries.shape[main_axis]] + index_at[main_axis + 1:]
    return entries.at[tuple(index_at)].set(low).at[tuple(neighbour)].set(largest)


def levels(rng, shape, pieces, smallest, top_value):
    def one(position, blocks):
        steps = jax.random.uniform(jax.random.fold_in(jax.random.fold_in(rng, 6), position), (blocks,), jnp.float32, smallest / len(pieces), top_value / len(pieces))
        return jnp.repeat(jnp.exp(steps), shape[position] // blocks).reshape((-1,) + (1,) * (len(shape) - position - 1))

    loudness = one(*pieces[0])
    for cut in pieces[1:]:
        loudness = loudness * one(*cut)
    return loudness


def gaussian(key, shape, spread, reach, cuts=(), held_as=jnp.bfloat16):
    values = jax.random.normal(key, shape, jnp.float32) * spread
    if len(cuts) > 0:
        values = levels(key, shape, cuts, -0.22, 0.18) * values
    return jnp.clip(values, min=-reach, max=reach).astype(held_as)


def setup_inputs(seed: int = 0) -> dict:
    arg_keys = jax.random.split(jax.random.key(seed), 9)
    return {
        "tokens_in": gaussian(arg_keys[0], (TOKENS, D), 1.0, 6.0, ((0, 128),)),
        "out_grad": gaussian(arg_keys[1], (TOKENS, D), 1.0, 6.0, ((0, 128),)),
        "expert_ids": draw_expert_ids(jax.random.fold_in(arg_keys[8], 71), 0),
        "router_codes": set_ends(jax.random.randint(arg_keys[3], (TOKENS, TOPK), 1, 65), jax.random.fold_in(arg_keys[3], 1), 1, 64).astype(jnp.int32),
        "amax_history": set_ends(jax.random.randint(arg_keys[4], (EXPERTS, HIST), -2, 3), jax.random.fold_in(arg_keys[4], 1), -2, 2).astype(jnp.int32),
        "w_gate": gaussian(arg_keys[5], (EXPERTS, D, H), D ** -0.5, 0.09375, ((0, 16),)),
        "w_up": gaussian(arg_keys[6], (EXPERTS, D, H), D ** -0.5, 0.09375, ((0, 16),)),
        "w_down": gaussian(arg_keys[7], (EXPERTS, H, D), H ** -0.5, 0.21875, ((0, 16),)),
    }


saturation = 2.0
weight_factor = 1.0 / 64.0


def scales_of(history):
    return jnp.exp2(-jnp.max(history, axis=1).astype(jnp.float32))


def slots_of(ids, experts, cap):
    flat = ids.reshape(-1)
    marks = (flat[:, None] == jnp.arange(experts, dtype=jnp.int32)[None, :]).astype(jnp.int32)
    before = jnp.cumsum(marks, axis=0) - marks
    slot = jnp.sum(before * marks, axis=1)
    return (flat * cap + slot).astype(jnp.int32)


def quantize(grad, codes, ids, scales):
    experts = scales.shape[0]
    marks = ids[:, :, None] == jnp.arange(experts, dtype=jnp.int32)[None, None, :]
    chosen = jnp.sum(jnp.where(marks, scales[None, None, :], 0.0), axis=2)
    factor = codes.astype(jnp.float32) / 64.0 * chosen
    values = grad.astype(jnp.float32)[:, None, :] * factor[:, :, None]
    return jnp.clip(values, -saturation, saturation).astype(jnp.bfloat16)


def backward_rows(rows_x, rows_q, scale, wg, wu, wd):
    gate = jnp.dot(rows_x, wg, preferred_element_type=jnp.float32)
    up = jnp.dot(rows_x, wu, preferred_element_type=jnp.float32)
    sig = jax.nn.sigmoid(gate)
    act = gate * sig
    hidden = (act * up).astype(jnp.bfloat16)
    unscaled = (rows_q.astype(jnp.float32) / scale).astype(jnp.bfloat16)
    d_hidden = lax.dot_general(unscaled, wd, (((1,), (1,)), ((), ())), preferred_element_type=jnp.float32)
    d_gate = (d_hidden * up * sig * (1.0 + gate * (1.0 - sig))).astype(jnp.bfloat16)
    d_up = (d_hidden * act).astype(jnp.bfloat16)
    return d_gate, d_up, hidden, unscaled


def input_rows(d_gate, d_up, wg, wu):
    first = lax.dot_general(d_gate, wg, (((1,), (1,)), ((), ())), preferred_element_type=jnp.float32)
    second = lax.dot_general(d_up, wu, (((1,), (1,)), ((), ())), preferred_element_type=jnp.float32)
    return (first + second).astype(jnp.bfloat16)


def inner_rows(left, right):
    return lax.dot_general(left, right, (((0,), (0,)), ((), ())), preferred_element_type=jnp.float32)


def rounded(value):
    return lax.optimization_barrier(value.astype(jnp.bfloat16)).astype(jnp.float32)


def reference(tokens_in, out_grad, expert_ids, router_codes, amax_history, w_gate, w_up, w_down):
    scales = scales_of(amax_history)
    sources = EXPERTS
    group_x = tokens_in.reshape(N_DP, sources, TOK_DEV, D)
    group_g = out_grad.reshape(N_DP, sources, TOK_DEV, D)
    group_ids = expert_ids.reshape(N_DP, sources, TOK_DEV, TOPK)
    group_codes = router_codes.reshape(N_DP, sources, TOK_DEV, TOPK)

    def place(rows, dest):
        return jnp.zeros((EXPERTS * CAP, D), jnp.bfloat16).at[dest].set(rows)

    def per_expert(items):
        rows_x, rows_q, scale, wg, wu, wd = items
        d_gate, d_up, hidden, unscaled = backward_rows(rows_x, rows_q, scale, wg, wu, wd)
        back = input_rows(d_gate, d_up, wg, wu)
        return back, inner_rows(rows_x, d_gate), inner_rows(rows_x, d_up), inner_rows(hidden, unscaled)

    def group_step(carry, items):
        xs, gs, ids, codes = items
        dest = jax.vmap(lambda one: slots_of(one, EXPERTS, CAP))(ids)
        quant = jax.vmap(lambda a, b, c: quantize(a, b, c, scales))(gs, codes, ids)
        quant = quant.reshape(sources, TOK_DEV * TOPK, D)
        repeated = jnp.repeat(xs, TOPK, axis=1)
        xbuf = jax.vmap(place)(repeated, dest)
        qbuf = jax.vmap(place)(quant, dest)
        xe = xbuf.reshape(sources, EXPERTS, CAP, D).transpose(1, 0, 2, 3).reshape(EXPERTS, sources * CAP, D)
        qe = qbuf.reshape(sources, EXPERTS, CAP, D).transpose(1, 0, 2, 3).reshape(EXPERTS, sources * CAP, D)
        back, dwg, dwu, dwd = lax.map(per_expert, (xe, qe, scales, w_gate, w_up, w_down))
        back = back.reshape(EXPERTS, sources, CAP, D).transpose(1, 0, 2, 3).reshape(sources, EXPERTS * CAP, D)
        picked = jax.vmap(lambda rows, idx: rows[idx])(back, dest)
        grads = jnp.sum(picked.astype(jnp.float32).reshape(sources, TOK_DEV, TOPK, D), axis=2).astype(jnp.bfloat16)
        carry = (carry[0] + rounded(dwg), carry[1] + rounded(dwu), carry[2] + rounded(dwd))
        return carry, grads

    init = (jnp.zeros((EXPERTS, D, H), jnp.float32), jnp.zeros((EXPERTS, D, H), jnp.float32),
            jnp.zeros((EXPERTS, H, D), jnp.float32))
    sums, grads = lax.scan(group_step, init, (group_x, group_g, group_ids, group_codes))
    grad_tokens = grads.reshape(TOKENS, D)
    return (grad_tokens, (sums[0] * weight_factor).astype(jnp.bfloat16),
            (sums[1] * weight_factor).astype(jnp.bfloat16), (sums[2] * weight_factor).astype(jnp.bfloat16))
```

```python
import jax
import jax.numpy as jnp
from jax import lax
from jax.experimental import pallas as pl
from jax.experimental.pallas import tpu as pltpu
from jax.sharding import PartitionSpec as P

saturation = 2.0
weight_factor = 1.0 / 64.0
MIB = 1024 * 1024


def params(limit):
    return pltpu.CompilerParams(vmem_limit_bytes=limit * MIB)


def cost(flops, nbytes):
    return pl.CostEstimate(flops=int(flops), bytes_accessed=int(nbytes), transcendentals=0)


def dot_nn(a, b):
    return lax.dot_general(a, b, (((1,), (0,)), ((), ())), preferred_element_type=jnp.float32)


def dot_nt(a, b):
    return lax.dot_general(a, b, (((1,), (1,)), ((), ())), preferred_element_type=jnp.float32)


def dot_tn(a, b):
    return lax.dot_general(a, b, (((0,), (0,)), ((), ())), preferred_element_type=jnp.float32)


def pack(tokens, grad, ids, codes, history, n_dp):
    tok, width = tokens.shape
    experts = history.shape[0]
    cap = tok * 2 * 2 // experts
    slots = experts * cap
    part = width // n_dp
    half = part // 2
    step = 4 * half
    nx = width // step
    nq = width // 2 // step

    def body(ids_ref, codes_ref, hist_ref, x_ref, g_ref, first_ref, second_ref, sel_ref, fac_ref):
        j = pl.program_id(0)

        @pl.when(j == 0)
        def _():
            rows = lax.broadcasted_iota(jnp.int32, (tok, tok), 0)
            cols = lax.broadcasted_iota(jnp.int32, (tok, tok), 1)
            eye = rows == cols

            def as_row(column):
                wide = jnp.broadcast_to(column.astype(jnp.float32), (tok, tok))
                return jnp.sum(jnp.where(eye, wide, 0.0), axis=0, keepdims=True)

            earlier = (rows < cols).astype(jnp.bfloat16)
            expert = lax.broadcasted_iota(jnp.int32, (experts, tok), 0)
            magnitude = jnp.max(hist_ref[...], axis=1, keepdims=True)
            scale = jnp.zeros((experts, 1), jnp.float32)
            inverse = jnp.zeros((experts, 1), jnp.float32)
            for value in range(-2, 3):
                scale = jnp.where(magnitude == value, 2.0**-value, scale)
                inverse = jnp.where(magnitude == value, 2.0**value, inverse)
            id_rows = [as_row(ids_ref[:, k : k + 1]).astype(jnp.int32) for k in range(2)]
            marks = [expert == row for row in id_rows]
            count = (marks[0] | marks[1]).astype(jnp.float32)
            before = dot_nn(count.astype(jnp.bfloat16), earlier)
            slot = lax.broadcasted_iota(jnp.int32, (slots, tok), 0)
            select = jnp.zeros((slots, tok), jnp.float32)
            factor = jnp.zeros((slots, tok), jnp.float32)
            unscale = jnp.zeros((slots, tok), jnp.float32)
            for k in range(2):
                place = jnp.sum(jnp.where(marks[k], before, 0.0), axis=0, keepdims=True)
                dest = id_rows[k] * cap + place.astype(jnp.int32)
                chosen = jnp.sum(jnp.where(marks[k], scale, 0.0), axis=0, keepdims=True)
                back = jnp.sum(jnp.where(marks[k], inverse, 0.0), axis=0, keepdims=True)
                weight = as_row(codes_ref[:, k : k + 1]) / 64.0 * chosen
                hit = slot == dest
                select = jnp.where(hit, 1.0, select)
                factor = jnp.where(hit, weight, factor)
                unscale = jnp.where(hit, back, unscale)
            sel_ref[...] = select.astype(jnp.bfloat16)
            fac_ref[0] = jnp.sum(factor, axis=1, keepdims=True)
            fac_ref[1] = jnp.sum(unscale, axis=1, keepdims=True)

        @pl.when(j < nx)
        def _():
            first_ref[...] = dot_nn(sel_ref[...], x_ref[...]).astype(jnp.bfloat16)

        def gradient(base, out_ref):
            for r in range(4):
                start = pl.multiple_of(base + r * part, half)
                picked = dot_nn(sel_ref[...], g_ref[:, pl.ds(start, half)])
                clipped = jnp.clip(picked * fac_ref[0], -saturation, saturation)
                rounded = clipped.astype(jnp.bfloat16).astype(jnp.float32)
                out_ref[:, r * half : (r + 1) * half] = (rounded * fac_ref[1]).astype(jnp.bfloat16)

        @pl.when((j >= nx) & (j < nx + nq))
        def _():
            gradient((j - nx) * 4 * part, first_ref)

        @pl.when(j >= nx + nq)
        def _():
            gradient((j - nx - nq) * 4 * part + half, second_ref)

    whole = lambda shape: pl.BlockSpec(shape, lambda j: (0,) * len(shape))
    return pl.pallas_call(
        body,
        grid=(nx + 2 * nq,),
        in_specs=[
            whole(ids.shape),
            whole(codes.shape),
            whole(history.shape),
            pl.BlockSpec((tok, step), lambda j: (0, jnp.minimum(j, nx - 1))),
            whole(grad.shape),
        ],
        out_specs=[
            pl.BlockSpec((slots, step), lambda j: (0, jnp.minimum(j, nx + nq - 1))),
            pl.BlockSpec((slots, step), lambda j: (0, jnp.maximum(j - nx - nq, 0))),
            whole((slots, tok)),
        ],
        out_shape=[
            jax.ShapeDtypeStruct((slots, width + width // 2), jnp.bfloat16),
            jax.ShapeDtypeStruct((slots, width // 2), jnp.bfloat16),
            jax.ShapeDtypeStruct((slots, tok), jnp.bfloat16),
        ],
        scratch_shapes=[pltpu.VMEM((2, slots, 1), jnp.float32)],
        compiler_params=params(32),
        cost_estimate=cost(4 * slots * tok * width, 12 * slots * width // 3),
        name="pack",
    )(ids, codes, history, tokens, grad)


def forward(first, w_gate, w_up):
    rows = first.shape[0]
    width, units = w_gate.shape[1:]
    block = 256

    def body(x_ref, wg_ref, wu_ref, hidden_ref, for_gate_ref, for_up_ref):
        gate = dot_nn(x_ref[...], wg_ref[...])
        up = dot_nn(x_ref[...], wu_ref[...])
        sig = jax.nn.sigmoid(gate)
        act = gate * sig
        hidden_ref[...] = (act * up).astype(jnp.bfloat16)
        for_gate_ref[...] = up * sig * (1.0 + gate * (1.0 - sig))
        for_up_ref[...] = act

    out = pl.BlockSpec((rows, block), lambda j: (0, j))
    weight = pl.BlockSpec((None, width, block), lambda j: (0, 0, j))
    return pl.pallas_call(
        body,
        grid=(units // block,),
        in_specs=[pl.BlockSpec((rows, width), lambda j: (0, 0)), weight, weight],
        out_specs=[out, out, out],
        out_shape=[
            jax.ShapeDtypeStruct((rows, units), jnp.bfloat16),
            jax.ShapeDtypeStruct((rows, units), jnp.float32),
            jax.ShapeDtypeStruct((rows, units), jnp.float32),
        ],
        compiler_params=params(40),
        cost_estimate=cost(4 * rows * width * units, 4 * width * units + 2 * rows * width),
        name="forward",
    )(first, w_gate, w_up)


def hidden_grad(buf, offset, w_down, which, n_dp, more=None):
    rows = buf.shape[0]
    units, width = w_down.shape[1:]
    part = width // n_dp
    half = part // 2
    block = 256

    def body(q_ref, wd_ref, *refs):
        total = None
        for i in range(n_dp):
            start = i * part + which * half
            term = dot_nt(q_ref[:, i * half : (i + 1) * half], wd_ref[:, start : start + half])
            total = term if total is None else total + term
        if more is None:
            refs[0][...] = total
        else:
            total = total + refs[0][...]
            refs[3][...] = (total * refs[1][...]).astype(jnp.bfloat16)
            refs[4][...] = (total * refs[2][...]).astype(jnp.bfloat16)

    tile = pl.BlockSpec((rows, block), lambda j: (0, j))
    extra = [] if more is None else list(more)
    outs = (
        [jax.ShapeDtypeStruct((rows, units), jnp.float32)]
        if more is None
        else [jax.ShapeDtypeStruct((rows, units), jnp.bfloat16)] * 2
    )
    return pl.pallas_call(
        body,
        grid=(units // block,),
        in_specs=[
            pl.BlockSpec((rows, width // 2), lambda j: (0, offset)),
            pl.BlockSpec((None, block, width), lambda j: (0, j, 0)),
        ]
        + [tile] * len(extra),
        out_specs=[tile] * len(outs),
        out_shape=outs,
        compiler_params=params(32),
        cost_estimate=cost(rows * width * units, 2 * width * units + rows * width),
        name="hidden_grad",
    )(buf, w_down, *extra)


def weight_part(kind, buf, base, width, other, places, received=None):
    rows = buf.shape[0]
    units = other.shape[1]
    shape = (width, units) if kind == "rows" else (units, width)
    half = shape[0] // 2

    def product(buf_ref, other_ref):
        if kind == "rows":
            return dot_tn(buf_ref[...], other_ref[...])
        return dot_tn(other_ref[...], buf_ref[...])

    def plain(places_ref, buf_ref, other_ref, out_ref):
        out_ref[...] = product(buf_ref, other_ref).astype(jnp.bfloat16)

    def summed(places_ref, buf_ref, other_ref, in_ref, fwd_ref, bwd_ref, keep1_ref, keep3_ref, own_ref):
        j = pl.program_id(0)
        total = product(buf_ref, other_ref) + in_ref[...].astype(jnp.float32)
        total = total.astype(jnp.bfloat16)
        low, high = total[:half], total[half:]

        @pl.when(j == 0)
        def _():
            fwd_ref[0] = low
            bwd_ref[0] = high

        @pl.when(j == 1)
        def _():
            keep1_ref[...] = low
            fwd_ref[1] = high

        @pl.when(j == 2)
        def _():
            bwd_ref[1] = low
            keep3_ref[...] = high

        @pl.when(j == 3)
        def _():
            own_ref[...] = total

    ins = [
        pl.BlockSpec((rows, width), lambda j, at: (0, base + at[j])),
        pl.BlockSpec((rows, units), lambda j, at: (0, 0)),
    ]
    flat = jnp.bfloat16
    if received is None:
        outs = pl.BlockSpec((None,) + shape, lambda j, at: (j, 0, 0))
        out_shape = jax.ShapeDtypeStruct((4,) + shape, flat)
        args = (buf, other)
    else:
        ins.append(pl.BlockSpec((None,) + shape, lambda j, at: (j, 0, 0)))
        shapes = [(2, half, shape[1])] * 2 + [(half, shape[1])] * 2 + [shape]
        outs = [pl.BlockSpec(s, lambda j, at, n=len(s): (0,) * n) for s in shapes]
        out_shape = [jax.ShapeDtypeStruct(s, flat) for s in shapes]
        args = (buf, other, received)
    return pl.pallas_call(
        plain if received is None else summed,
        grid_spec=pltpu.PrefetchScalarGridSpec(
            num_scalar_prefetch=1, grid=(4,), in_specs=ins, out_specs=outs
        ),
        out_shape=out_shape,
        compiler_params=params(32),
        cost_estimate=cost(8 * rows * width * units, 12 * width * units + 8 * rows * width),
        name="weight_part",
    )(places, *args)


def input_rows(d_gate, d_up, w_gate, w_up):
    rows, units = d_gate.shape
    width = w_gate.shape[1]
    block = 512

    def body(dg_ref, du_ref, wg_ref, wu_ref, out_ref):
        total = dot_nt(dg_ref[...], wg_ref[...]) + dot_nt(du_ref[...], wu_ref[...])
        out_ref[...] = total.astype(jnp.bfloat16)

    whole = pl.BlockSpec((rows, units), lambda j: (0, 0))
    weight = pl.BlockSpec((None, block, units), lambda j: (0, j, 0))
    return pl.pallas_call(
        body,
        grid=(width // block,),
        in_specs=[whole, whole, weight, weight],
        out_specs=pl.BlockSpec((rows, block), lambda j: (0, j)),
        out_shape=jax.ShapeDtypeStruct((rows, width), jnp.bfloat16),
        compiler_params=params(32),
        cost_estimate=cost(4 * rows * width * units, 4 * width * units + 2 * rows * width),
        name="input_rows",
    )(d_gate, d_up, w_gate, w_up)


def combine(select, returned):
    slots, tok = select.shape
    width = returned.shape[1]
    block = 1024

    def body(sel_ref, in_ref, out_ref):
        out_ref[...] = dot_tn(sel_ref[...], in_ref[...]).astype(jnp.bfloat16)

    return pl.pallas_call(
        body,
        grid=(width // block,),
        in_specs=[
            pl.BlockSpec((slots, tok), lambda j: (0, 0)),
            pl.BlockSpec((slots, block), lambda j: (0, j)),
        ],
        out_specs=pl.BlockSpec((tok, block), lambda j: (0, j)),
        out_shape=jax.ShapeDtypeStruct((tok, width), jnp.bfloat16),
        compiler_params=params(32),
        cost_estimate=cost(2 * slots * tok * width, 2 * slots * width),
        name="combine",
    )(select, returned)


def shards(tokens_in, out_grad, expert_ids, router_codes, amax_history, w_gate, w_up, w_down):
    n_dp = lax.axis_size("dp")
    peers = lax.axis_size("expert")
    width = tokens_in.shape[1]
    experts = amax_history.shape[0]
    part = width // n_dp
    half = part // 2
    place = lax.axis_index("dp")
    z, core = place // 2, place % 2
    n_z = n_dp // 2
    order = (z + jnp.array([2, 1, 3, 0], jnp.int32)) % n_z * 2
    theirs = order + (1 - core)
    ours = order + core

    swap = [(i, i ^ 1) for i in range(n_dp)]
    ahead = [(i, (i + 2) % n_dp) for i in range(n_dp)]
    behind = [(i, (i - 2) % n_dp) for i in range(n_dp)]

    def exchange(buf):
        blocks = buf.reshape(peers, -1, buf.shape[1])
        out = lax.all_to_all(blocks, "expert", split_axis=0, concat_axis=0, tiled=True)
        return out.reshape(buf.shape)

    def wide(value):
        return value.astype(jnp.float32)

    def reduced(kind, buf, base, cut, other):
        mine = weight_part(kind, buf, base, cut, other, theirs)
        got = lax.ppermute(mine, "dp", swap)
        fwd, bwd, keep1, keep3, own = weight_part(kind, buf, base, cut, other, ours, got)
        from_behind = lax.ppermute(fwd, "dp", ahead)
        from_ahead = lax.ppermute(bwd, "dp", behind)
        fwd2 = (wide(keep1) + wide(from_behind[0])).astype(jnp.bfloat16)
        bwd2 = (wide(keep3) + wide(from_ahead[0])).astype(jnp.bfloat16)
        low = lax.ppermute(fwd2, "dp", ahead)
        high = lax.ppermute(bwd2, "dp", behind)
        cut_at = own.shape[0] // 2
        first = wide(own[:cut_at]) + wide(from_ahead[1]) + wide(low)
        second = wide(own[cut_at:]) + wide(from_behind[1]) + wide(high)
        total = jnp.concatenate([first, second], axis=0)
        return (total * weight_factor).astype(jnp.bfloat16)

    first, second, select = pack(
        tokens_in, out_grad, expert_ids, router_codes, amax_history, n_dp
    )
    first = exchange(first)
    second = exchange(second)
    hidden, for_gate, for_up = forward(first, w_gate, w_up)
    down_a = reduced("columns", first, width // half, half, hidden)
    (d_hidden,) = hidden_grad(first, 2, w_down, 0, n_dp)
    down_b = reduced("columns", second, 0, half, hidden)
    d_gate, d_up = hidden_grad(second, 0, w_down, 1, n_dp, (d_hidden, for_gate, for_up))
    grad_gate = reduced("rows", first, 0, part, d_gate)
    grad_up = reduced("rows", first, 0, part, d_up)
    back = exchange(input_rows(d_gate, d_up, w_gate, w_up))
    grad_tokens = combine(select, back)
    grad_down = jnp.concatenate([down_a, down_b], axis=1)
    return (grad_tokens, grad_gate[None], grad_up[None], grad_down[None])


def solution(mesh):
    return jax.shard_map(
        shards,
        mesh=mesh,
        in_specs=(
            P(("dp", "expert"), None),
            P(("dp", "expert"), None),
            P(("dp", "expert"), None),
            P(("dp", "expert"), None),
            P(),
            P("expert", None, None),
            P("expert", None, None),
            P("expert", None, None),
        ),
        out_specs=(
            P(("dp", "expert"), None),
            P("expert", "dp", None),
            P("expert", "dp", None),
            P("expert", None, "dp"),
        ),
        check_vma=False,
    )
```

```python
import jax
import jax.numpy as jnp
from jax import lax
from jax.experimental import pallas as pl
from jax.experimental.pallas import tpu as pltpu
from jax.sharding import PartitionSpec as P

saturation = 2.0
weight_factor = 1.0 / 64.0
MIB = 1024 * 1024


def params(limit):
    return pltpu.CompilerParams(vmem_limit_bytes=limit * MIB)


def cost(flops, nbytes):
    return pl.CostEstimate(flops=int(flops), bytes_accessed=int(nbytes), transcendentals=0)


def dot_nn(a, b):
    return lax.dot_general(a, b, (((1,), (0,)), ((), ())), preferred_element_type=jnp.float32)


def dot_nt(a, b):
    return lax.dot_general(a, b, (((1,), (1,)), ((), ())), preferred_element_type=jnp.float32)


def dot_tn(a, b):
    return lax.dot_general(a, b, (((0,), (0,)), ((), ())), preferred_element_type=jnp.float32)


ANY = pl.BlockSpec(memory_space=pl.ANY)


LONG = 1000
MICROS = {'oD': 5, 'hg': 5, 'wD': 5, 'i0': 100, 'oG': 100, 'nD': 100, 'oU': 100, 'wG': 100, 'wU': 100, 'nG': 100, 'fD': 100, 'nU': 100, 'fG': 100, 'fU': 100}


def takes(micros):
    return cost(micros * 1.15e9, 1e6)


def in_hbm(value):
    return pltpu.with_memory_space_constraint(value, pltpu.HBM)


def ordered(body, n_read, n_after):
    if n_after == 0:
        return body
    return lambda *refs: body(*refs[:n_read], *refs[n_read + n_after :])


def in_vmem(value):
    return pltpu.with_memory_space_constraint(value, pltpu.VMEM)


def pack(tokens, grad, ids, codes, history, place):
    tok, width = tokens.shape
    experts = history.shape[1]
    cap = tok * 2 * 2 // experts
    slots = experts * cap
    step = 1024
    nx = width // step

    def body(ids_ref, codes_ref, hist_ref, x_ref, g_ref, out_ref, sel_ref, fac_ref):
        j = pl.program_id(0)

        @pl.when(j == 0)
        def _():
            rows = lax.broadcasted_iota(jnp.int32, (tok, tok), 0)
            cols = lax.broadcasted_iota(jnp.int32, (tok, tok), 1)
            earlier = (rows < cols).astype(jnp.bfloat16)
            expert = lax.broadcasted_iota(jnp.int32, (experts, tok), 0)
            largest = jnp.max(hist_ref[...], axis=0, keepdims=True).astype(jnp.float32)
            diagonal = lax.broadcasted_iota(
                jnp.int32, (experts, experts), 0
            ) == lax.broadcasted_iota(jnp.int32, (experts, experts), 1)
            wide = jnp.broadcast_to(largest, (experts, experts))
            magnitude = jnp.sum(jnp.where(diagonal, wide, 0.0), axis=1, keepdims=True)
            scale = jnp.zeros((experts, 1), jnp.float32)
            inverse = jnp.zeros((experts, 1), jnp.float32)
            for value in range(-2, 3):
                scale = jnp.where(magnitude == value, 2.0**-value, scale)
                inverse = jnp.where(magnitude == value, 2.0**value, inverse)
            id_rows = [ids_ref[k : k + 1, :] for k in range(2)]
            marks = [expert == row for row in id_rows]
            count = (marks[0] | marks[1]).astype(jnp.float32)
            before = dot_nn(count.astype(jnp.bfloat16), earlier)
            slot = lax.broadcasted_iota(jnp.int32, (slots, tok), 0)
            select = jnp.zeros((slots, tok), jnp.float32)
            factor = jnp.zeros((slots, tok), jnp.float32)
            unscale = jnp.zeros((slots, tok), jnp.float32)
            for k in range(2):
                place = jnp.sum(jnp.where(marks[k], before, 0.0), axis=0, keepdims=True)
                dest = id_rows[k] * cap + place.astype(jnp.int32)
                chosen = jnp.sum(jnp.where(marks[k], scale, 0.0), axis=0, keepdims=True)
                back = jnp.sum(jnp.where(marks[k], inverse, 0.0), axis=0, keepdims=True)
                weight = codes_ref[k : k + 1, :].astype(jnp.float32) / 64.0 * chosen
                hit = slot == dest
                select = jnp.where(hit, 1.0, select)
                factor = jnp.where(hit, weight, factor)
                unscale = jnp.where(hit, back, unscale)
            sel_ref[...] = select.astype(jnp.bfloat16)
            fac_ref[0] = jnp.sum(factor, axis=1, keepdims=True)
            fac_ref[1] = jnp.sum(unscale, axis=1, keepdims=True)

        @pl.when(j < nx)
        def _():
            out_ref[...] = dot_nn(sel_ref[...], x_ref[...]).astype(jnp.bfloat16)

        @pl.when(j >= nx)
        def _():
            picked = dot_nn(sel_ref[...], g_ref[...])
            clipped = jnp.clip(picked * fac_ref[0], -saturation, saturation)
            rounded = clipped.astype(jnp.bfloat16).astype(jnp.float32)
            out_ref[...] = (rounded * fac_ref[1]).astype(jnp.bfloat16)

    whole = lambda shape: pl.BlockSpec(shape, lambda j: (0,) * len(shape))
    return pl.pallas_call(
        ordered(body, 5, 1),
        grid=(2 * nx,),
        in_specs=[
            whole(ids.shape),
            whole(codes.shape),
            whole(history.shape),
            pl.BlockSpec((tok, step), lambda j: (0, jnp.minimum(j, nx - 1))),
            pl.BlockSpec((tok, step), lambda j: (0, jnp.maximum(j - nx, 0))),
            ANY,
        ],
        out_specs=[pl.BlockSpec((slots, step), lambda j: (0, j)), whole((slots, tok))],
        out_shape=[
            pltpu.HBM((slots, 2 * width), jnp.bfloat16),
            jax.ShapeDtypeStruct((slots, tok), jnp.bfloat16),
        ],
        scratch_shapes=[pltpu.VMEM((2, slots, 1), jnp.float32)],
        compiler_params=params(14),
        cost_estimate=takes(10),
        name="pack",
    )(in_hbm(ids), in_hbm(codes), in_hbm(history), in_hbm(tokens), in_hbm(grad), place)


def forward(first, w_gate, w_up):
    rows = first.shape[0]
    width, units = w_gate.shape[1:]
    block = 256

    def body(x_ref, wg_ref, wu_ref, hidden_ref, for_gate_ref, for_up_ref):
        gate = dot_nn(x_ref[...], wg_ref[...])
        up = dot_nn(x_ref[...], wu_ref[...])
        sig = jax.nn.sigmoid(gate)
        act = gate * sig
        hidden_ref[...] = (act * up).astype(jnp.bfloat16)
        for_gate_ref[...] = up * sig * (1.0 + gate * (1.0 - sig))
        for_up_ref[...] = act

    out = pl.BlockSpec((rows, block), lambda j: (0, j))
    weight = pl.BlockSpec((None, width, block), lambda j: (0, 0, j))
    return pl.pallas_call(
        body,
        grid=(units // block,),
        in_specs=[pl.BlockSpec((rows, width), lambda j: (0, 0)), weight, weight],
        out_specs=[out, out, out],
        out_shape=[
            jax.ShapeDtypeStruct((rows, units), jnp.bfloat16),
            jax.ShapeDtypeStruct((rows, units), jnp.float32),
            jax.ShapeDtypeStruct((rows, units), jnp.float32),
        ],
        compiler_params=params(24),
        cost_estimate=takes(10),
        name="forward",
    )(in_hbm(first), in_vmem(w_gate), in_vmem(w_up))


def hidden_grad(buf, offset, w_down, for_gate, for_up, after=(), micros=LONG):
    rows = buf.shape[0]
    units, width = w_down.shape[1:]
    block = 256

    def body(q_ref, wd_ref, for_gate_ref, for_up_ref, d_gate_ref, d_up_ref):
        total = dot_nt(q_ref[...], wd_ref[...])
        d_gate_ref[...] = (total * for_gate_ref[...]).astype(jnp.bfloat16)
        d_up_ref[...] = (total * for_up_ref[...]).astype(jnp.bfloat16)

    tile = pl.BlockSpec((rows, block), lambda j: (0, j))
    return pl.pallas_call(
        ordered(body, 4, len(after)),
        grid=(units // block,),
        in_specs=[
            pl.BlockSpec((rows, width), lambda j: (0, offset)),
            pl.BlockSpec((None, block, width), lambda j: (0, j, 0)),
            tile,
            tile,
        ]
        + [ANY] * len(after),
        out_specs=[tile] * 2,
        out_shape=[jax.ShapeDtypeStruct((rows, units), jnp.bfloat16)] * 2,
        compiler_params=params(20),
        cost_estimate=takes(micros),
        name="hidden_grad",
    )(in_hbm(buf), in_vmem(w_down), for_gate, for_up, *after)


def weight_part(kind, buf, base, width, other, place, own, received=None, after=(), micros=LONG):
    rows = buf.shape[0]
    units = other.shape[1]
    shape = (width, units) if kind == "rows" else (units, width)
    half = shape[0] // 2

    def product(buf_ref, other_ref):
        if kind == "rows":
            return dot_tn(buf_ref[...], other_ref[...])
        return dot_tn(other_ref[...], buf_ref[...])

    def plain(place_ref, buf_ref, other_ref, out_ref):
        out_ref[...] = product(buf_ref, other_ref).astype(jnp.bfloat16)

    def summed(place_ref, buf_ref, other_ref, in_ref, fwd_ref, bwd_ref, keep1_ref, keep3_ref, own_ref):
        j = pl.program_id(0)
        total = product(buf_ref, other_ref) + in_ref[...].astype(jnp.float32)
        total = total.astype(jnp.bfloat16)
        low, high = total[:half], total[half:]

        @pl.when(j == 0)
        def _():
            fwd_ref[0] = low
            bwd_ref[0] = high

        @pl.when(j == 1)
        def _():
            keep1_ref[...] = low
            fwd_ref[1] = high

        @pl.when(j == 2)
        def _():
            own_ref[...] = total

        @pl.when(j == 3)
        def _():
            bwd_ref[1] = low
            keep3_ref[...] = high

    def column(j, at):
        z, core = at[0] // 2, at[0] % 2
        wanted = core if own else 1 - core
        return (0, base + (z + 6 - j) % 4 * 2 + wanted)

    ins = [
        pl.BlockSpec((rows, width), column),
        pl.BlockSpec((rows, units), lambda j, at: (0, 0)),
    ]
    flat = jnp.bfloat16
    if received is None:
        outs = pl.BlockSpec((None,) + shape, lambda j, at: (j, 0, 0))
        out_shape = jax.ShapeDtypeStruct((4,) + shape, flat)
        args = (in_hbm(buf), other)
    else:
        ins.append(pl.BlockSpec((None,) + shape, lambda j, at: (j, 0, 0)))
        shapes = [(2, half, shape[1])] * 2 + [(half, shape[1])] * 2 + [shape]
        outs = [pl.BlockSpec(s, lambda j, at, n=len(s): (0,) * n) for s in shapes]
        out_shape = [jax.ShapeDtypeStruct(s, flat) for s in shapes]
        args = (in_hbm(buf), other, received)
    ins += [ANY] * len(after)
    body = plain if received is None else summed
    return pl.pallas_call(
        ordered(body, 1 + len(args), len(after)),
        grid_spec=pltpu.PrefetchScalarGridSpec(
            num_scalar_prefetch=1, grid=(4,), in_specs=ins, out_specs=outs
        ),
        out_shape=out_shape,
        compiler_params=params(18),
        cost_estimate=takes(micros),
        name="weight_part",
    )(place, *args, *after)


def input_rows(d_gate, d_up, w_gate, w_up, after=(), micros=LONG):
    rows, units = d_gate.shape
    width = w_gate.shape[1]
    block = 512

    def body(dg_ref, du_ref, wg_ref, wu_ref, out_ref):
        total = dot_nt(dg_ref[...], wg_ref[...]) + dot_nt(du_ref[...], wu_ref[...])
        out_ref[...] = total.astype(jnp.bfloat16)

    whole = pl.BlockSpec((rows, units), lambda j: (0, 0))
    weight = pl.BlockSpec((None, block, units), lambda j: (0, j, 0))
    return pl.pallas_call(
        ordered(body, 4, len(after)),
        grid=(width // block,),
        in_specs=[whole, whole, weight, weight] + [ANY] * len(after),
        out_specs=pl.BlockSpec((rows, block), lambda j: (0, j)),
        out_shape=pltpu.HBM((rows, width), jnp.bfloat16),
        compiler_params=params(16),
        cost_estimate=takes(micros),
        name="input_rows",
    )(d_gate, d_up, in_vmem(w_gate), in_vmem(w_up), *after)


def passed_on(parts, hop, after=(), micros=LONG):
    half, width = parts[2].shape

    def body(up_ref, down_ref, low_ref, high_ref, fwd_ref, bwd_ref):
        fwd = up_ref[...].astype(jnp.float32) + low_ref[...].astype(jnp.float32)
        bwd = down_ref[...].astype(jnp.float32) + high_ref[...].astype(jnp.float32)
        fwd_ref[...] = fwd.astype(jnp.bfloat16)
        bwd_ref[...] = bwd.astype(jnp.bfloat16)

    block = half // 2
    flat = pl.BlockSpec((block, width), lambda j: (j, 0))
    first = pl.BlockSpec((None, block, width), lambda j: (0, j, 0))
    return pl.pallas_call(
        ordered(body, 4, len(after)),
        grid=(2,),
        in_specs=[flat, flat, first, first] + [ANY] * len(after),
        out_specs=[flat, flat],
        out_shape=[jax.ShapeDtypeStruct((half, width), jnp.bfloat16)] * 2,
        compiler_params=params(8),
        cost_estimate=takes(micros),
        name="passed_on",
    )(parts[2], parts[3], *hop, *after)


def finished(parts, hop, last, after=(), micros=LONG):
    half, width = parts[2].shape

    def body(own_ref, ahead_ref, behind_ref, low_ref, high_ref, out_ref):
        own = own_ref[...].astype(jnp.float32)

        def store(near_ref, far_ref):
            total = own + near_ref[...].astype(jnp.float32) + far_ref[...].astype(jnp.float32)
            out_ref[...] = (total * weight_factor).astype(jnp.bfloat16)

        @pl.when(pl.program_id(0) == 0)
        def _():
            store(ahead_ref, low_ref)

        @pl.when(pl.program_id(0) == 1)
        def _():
            store(behind_ref, high_ref)

    tile = pl.BlockSpec((half, width), lambda j: (j, 0))
    second = pl.BlockSpec((None, half, width), lambda j: (1, 0, 0))
    whole = pl.BlockSpec((half, width), lambda j: (0, 0))
    return pl.pallas_call(
        ordered(body, 5, len(after)),
        grid=(2,),
        in_specs=[tile, second, second, whole, whole] + [ANY] * len(after),
        out_specs=tile,
        out_shape=jax.ShapeDtypeStruct((2 * half, width), jnp.bfloat16),
        compiler_params=params(10),
        cost_estimate=takes(micros),
        name="finished",
    )(parts[4], hop[1], hop[0], *last, *after)


def combine(select, returned, after=()):
    slots, tok = select.shape
    width = returned.shape[1]
    block = 1024

    def body(sel_ref, in_ref, out_ref):
        out_ref[...] = dot_tn(sel_ref[...], in_ref[...]).astype(jnp.bfloat16)

    return pl.pallas_call(
        ordered(body, 2, len(after)),
        grid=(width // block,),
        in_specs=[
            pl.BlockSpec((slots, tok), lambda j: (0, 0)),
            pl.BlockSpec((slots, block), lambda j: (0, j)),
        ]
        + [ANY] * len(after),
        out_specs=pl.BlockSpec((tok, block), lambda j: (0, j)),
        out_shape=jax.ShapeDtypeStruct((tok, width), jnp.bfloat16),
        compiler_params=params(12),
        cost_estimate=takes(5),
        name="combine",
    )(select, in_hbm(returned), *after)


def shards(tokens_in, out_grad, expert_ids, router_codes, amax_history, w_gate, w_up, w_down):
    n_dp = lax.axis_size("dp")
    peers = lax.axis_size("expert")
    width = tokens_in.shape[1]
    experts = amax_history.shape[0]
    part = width // n_dp
    place = lax.axis_index("dp").astype(jnp.int32).reshape(1)

    swap = [(i, i ^ 1) for i in range(n_dp)]
    ahead = [(i, (i + 2) % n_dp) for i in range(n_dp)]
    behind = [(i, (i - 2) % n_dp) for i in range(n_dp)]

    def exchange(buf):
        blocks = buf.reshape(peers, -1, buf.shape[1])
        out = lax.all_to_all(blocks, "expert", split_axis=0, concat_axis=0, tiled=True)
        return out.reshape(buf.shape)

    def corner(value):
        return value[:16, :128] * 2

    def swapped(value):
        return lax.ppermute(value, "dp", swap)

    def one_hop(fwd, bwd):
        return lax.ppermute(fwd, "dp", ahead), lax.ppermute(bwd, "dp", behind)

    sent, select = pack(
        tokens_in, out_grad, expert_ids.T, router_codes.T, amax_history.T, place
    )
    rows = exchange(sent)
    hidden, for_gate, for_up = forward(rows, w_gate, w_up)
    down = ("columns", rows, width // part, part, hidden)
    other_down = weight_part(*down, place, False, micros=MICROS['oD'])
    d_gate, d_up = hidden_grad(rows, 1, w_down, for_gate, for_up, after=(other_down,), micros=MICROS['hg'])
    own_down = weight_part(*down, place, True, swapped(other_down), after=(d_gate,), micros=MICROS['wD'])
    hop_down = one_hop(*own_down[:2])
    rows_back = input_rows(
        d_gate, d_up, w_gate, w_up, after=(own_down[0], own_down[1]), micros=MICROS["i0"]
    )
    back = exchange(rows_back)
    gate = ("rows", rows, 0, part, d_gate)
    other_gate = weight_part(
        *gate, place, False, after=(corner(rows_back),), micros=MICROS["oG"]
    )
    next_down = passed_on(own_down, hop_down, after=(other_gate,), micros=MICROS["nD"])
    last_down = one_hop(*next_down)
    up = ("rows", rows, 0, part, d_up)
    other_up = weight_part(*up, place, False, after=next_down, micros=MICROS["oU"])
    own_gate = weight_part(
        *gate, place, True, swapped(other_gate), after=(other_up,), micros=MICROS["wG"]
    )
    hop_gate = one_hop(*own_gate[:2])
    own_up = weight_part(
        *up, place, True, swapped(other_up), after=own_gate[:2], micros=MICROS["wU"]
    )
    hop_up = one_hop(*own_up[:2])
    next_gate = passed_on(own_gate, hop_gate, after=own_up[:2], micros=MICROS["nG"])
    last_gate = one_hop(*next_gate)
    grad_down = finished(own_down, hop_down, last_down, after=next_gate, micros=MICROS["fD"])
    next_up = passed_on(own_up, hop_up, after=(grad_down,), micros=MICROS["nU"])
    last_up = one_hop(*next_up)
    grad_tokens = combine(select, back, after=next_up)
    grad_gate = finished(own_gate, hop_gate, last_gate, after=(grad_tokens,), micros=MICROS["fG"])
    grad_up = finished(own_up, hop_up, last_up, after=(grad_gate,), micros=MICROS["fU"])
    return (grad_tokens, grad_gate[None], grad_up[None], grad_down[None])


def solution(mesh):
    return jax.shard_map(
        shards,
        mesh=mesh,
        in_specs=(
            P(("dp", "expert"), None),
            P(("dp", "expert"), None),
            P(("dp", "expert"), None),
            P(("dp", "expert"), None),
            P(),
            P("expert", None, None),
            P("expert", None, None),
            P("expert", None, None),
        ),
        out_specs=(
            P(("dp", "expert"), None),
            P("expert", "dp", None),
            P("expert", "dp", None),
            P("expert", None, "dp"),
        ),
        check_vma=False,
    )
```

```python
import jax
import jax.numpy as jnp
from jax import lax
from jax.experimental import pallas as pl
from jax.experimental.pallas import tpu as pltpu
from jax.sharding import PartitionSpec as P

saturation = 2.0
weight_factor = 1.0 / 64.0
MIB = 1024 * 1024


def params(limit):
    return pltpu.CompilerParams(vmem_limit_bytes=limit * MIB)


def cost(flops, nbytes):
    return pl.CostEstimate(flops=int(flops), bytes_accessed=int(nbytes), transcendentals=0)


def dot_nn(a, b):
    return lax.dot_general(a, b, (((1,), (0,)), ((), ())), preferred_element_type=jnp.float32)


def dot_nt(a, b):
    return lax.dot_general(a, b, (((1,), (1,)), ((), ())), preferred_element_type=jnp.float32)


def dot_tn(a, b):
    return lax.dot_general(a, b, (((0,), (0,)), ((), ())), preferred_element_type=jnp.float32)


ANY = pl.BlockSpec(memory_space=pl.ANY)


LONG = 1000
MICROS = {'oD': 5, 'hg': 5, 'wD': 5, 'i0': 100, 'oG': 100, 'nD': 100, 'oU': 100, 'wG': 100, 'wU': 100, 'nG': 100, 'fD': 100, 'nU': 100, 'fG': 100, 'fU': 100}


def takes(micros):
    return cost(micros * 1.15e9, 1e6)


def in_hbm(value):
    return pltpu.with_memory_space_constraint(value, pltpu.HBM)


def ordered(body, n_read, n_after):
    if n_after == 0:
        return body
    return lambda *refs: body(*refs[:n_read], *refs[n_read + n_after :])


def in_vmem(value):
    return pltpu.with_memory_space_constraint(value, pltpu.VMEM)


def pack(tokens, grad, ids, codes, history, place):
    tok, width = tokens.shape
    experts = history.shape[1]
    cap = tok * 2 * 2 // experts
    slots = experts * cap
    step = 1024
    nx = width // step

    def body(ids_ref, codes_ref, hist_ref, x_ref, g_ref, out_ref, sel_ref, fac_ref):
        j = pl.program_id(0)

        @pl.when(j == 0)
        def _():
            rows = lax.broadcasted_iota(jnp.int32, (tok, tok), 0)
            cols = lax.broadcasted_iota(jnp.int32, (tok, tok), 1)
            earlier = (rows < cols).astype(jnp.bfloat16)
            expert = lax.broadcasted_iota(jnp.int32, (experts, tok), 0)
            largest = jnp.max(hist_ref[...], axis=0, keepdims=True).astype(jnp.float32)
            diagonal = lax.broadcasted_iota(
                jnp.int32, (experts, experts), 0
            ) == lax.broadcasted_iota(jnp.int32, (experts, experts), 1)
            wide = jnp.broadcast_to(largest, (experts, experts))
            magnitude = jnp.sum(jnp.where(diagonal, wide, 0.0), axis=1, keepdims=True)
            scale = jnp.zeros((experts, 1), jnp.float32)
            inverse = jnp.zeros((experts, 1), jnp.float32)
            for value in range(-2, 3):
                scale = jnp.where(magnitude == value, 2.0**-value, scale)
                inverse = jnp.where(magnitude == value, 2.0**value, inverse)
            id_rows = [ids_ref[k : k + 1, :] for k in range(2)]
            marks = [expert == row for row in id_rows]
            count = (marks[0] | marks[1]).astype(jnp.float32)
            before = dot_nn(count.astype(jnp.bfloat16), earlier)
            slot = lax.broadcasted_iota(jnp.int32, (slots, tok), 0)
            select = jnp.zeros((slots, tok), jnp.float32)
            factor = jnp.zeros((slots, tok), jnp.float32)
            unscale = jnp.zeros((slots, tok), jnp.float32)
            for k in range(2):
                place = jnp.sum(jnp.where(marks[k], before, 0.0), axis=0, keepdims=True)
                dest = id_rows[k] * cap + place.astype(jnp.int32)
                chosen = jnp.sum(jnp.where(marks[k], scale, 0.0), axis=0, keepdims=True)
                back = jnp.sum(jnp.where(marks[k], inverse, 0.0), axis=0, keepdims=True)
                weight = codes_ref[k : k + 1, :].astype(jnp.float32) / 64.0 * chosen
                hit = slot == dest
                select = jnp.where(hit, 1.0, select)
                factor = jnp.where(hit, weight, factor)
                unscale = jnp.where(hit, back, unscale)
            sel_ref[...] = select.astype(jnp.bfloat16)
            fac_ref[0] = jnp.sum(factor, axis=1, keepdims=True)
            fac_ref[1] = jnp.sum(unscale, axis=1, keepdims=True)

        @pl.when(j < nx)
        def _():
            out_ref[...] = dot_nn(sel_ref[...], x_ref[...]).astype(jnp.bfloat16)

        @pl.when(j >= nx)
        def _():
            picked = dot_nn(sel_ref[...], g_ref[...])
            clipped = jnp.clip(picked * fac_ref[0], -saturation, saturation)
            rounded = clipped.astype(jnp.bfloat16).astype(jnp.float32)
            out_ref[...] = (rounded * fac_ref[1]).astype(jnp.bfloat16)

    whole = lambda shape: pl.BlockSpec(shape, lambda j: (0,) * len(shape))
    return pl.pallas_call(
        ordered(body, 5, 1),
        grid=(2 * nx,),
        in_specs=[
            whole(ids.shape),
            whole(codes.shape),
            whole(history.shape),
            pl.BlockSpec((tok, step), lambda j: (0, jnp.minimum(j, nx - 1))),
            pl.BlockSpec((tok, step), lambda j: (0, jnp.maximum(j - nx, 0))),
            ANY,
        ],
        out_specs=[pl.BlockSpec((slots, step), lambda j: (0, j)), whole((slots, tok))],
        out_shape=[
            pltpu.VMEM((slots, 2 * width), jnp.bfloat16),
            jax.ShapeDtypeStruct((slots, tok), jnp.bfloat16),
        ],
        scratch_shapes=[pltpu.VMEM((2, slots, 1), jnp.float32)],
        compiler_params=params(14),
        cost_estimate=takes(10),
        name="pack",
    )(in_hbm(ids), in_hbm(codes), in_hbm(history), in_hbm(tokens), in_hbm(grad), place)


def forward(first, w_gate, w_up):
    rows = first.shape[0]
    width, units = w_gate.shape[1:]
    block = 1024
    steps = width // block

    def body(x_ref, wg_ref, wu_ref, hidden_ref, for_gate_ref, for_up_ref):
        k = pl.program_id(0)
        gate_part = dot_nn(x_ref[...], wg_ref[...])
        up_part = dot_nn(x_ref[...], wu_ref[...])

        @pl.when(k == 0)
        def _():
            for_up_ref[...] = gate_part
            for_gate_ref[...] = up_part

        @pl.when((k > 0) & (k < steps - 1))
        def _():
            for_up_ref[...] += gate_part
            for_gate_ref[...] += up_part

        @pl.when(k == steps - 1)
        def _():
            gate = for_up_ref[...] + gate_part
            up = for_gate_ref[...] + up_part
            sig = jax.nn.sigmoid(gate)
            act = gate * sig
            hidden_ref[...] = (act * up).astype(jnp.bfloat16)
            for_gate_ref[...] = up * sig * (1.0 + gate * (1.0 - sig))
            for_up_ref[...] = act

    out = pl.BlockSpec((rows, units), lambda k: (0, 0))
    weight = pl.BlockSpec((None, block, units), lambda k: (0, k, 0))
    return pl.pallas_call(
        body,
        grid=(steps,),
        in_specs=[pl.BlockSpec((rows, block), lambda k: (0, k)), weight, weight],
        out_specs=[out, out, out],
        out_shape=[
            jax.ShapeDtypeStruct((rows, units), jnp.bfloat16),
            jax.ShapeDtypeStruct((rows, units), jnp.float32),
            jax.ShapeDtypeStruct((rows, units), jnp.float32),
        ],
        compiler_params=params(28),
        cost_estimate=takes(10),
        name="forward",
    )(in_hbm(first), in_vmem(w_gate), in_vmem(w_up))


def hidden_grad(buf, offset, w_down, for_gate, for_up, after=(), micros=LONG):
    rows = buf.shape[0]
    units, width = w_down.shape[1:]
    block = 1024
    steps = width // block

    def body(q_ref, wd_ref, for_gate_ref, for_up_ref, d_gate_ref, d_up_ref, sum_ref):
        k = pl.program_id(0)
        part = dot_nt(q_ref[...], wd_ref[...])

        @pl.when(k == 0)
        def _():
            sum_ref[...] = part

        @pl.when((k > 0) & (k < steps - 1))
        def _():
            sum_ref[...] += part

        @pl.when(k == steps - 1)
        def _():
            total = sum_ref[...] + part
            d_gate_ref[...] = (total * for_gate_ref[...]).astype(jnp.bfloat16)
            d_up_ref[...] = (total * for_up_ref[...]).astype(jnp.bfloat16)

    tile = pl.BlockSpec((rows, units), lambda k: (0, 0))
    return pl.pallas_call(
        ordered(body, 4, len(after)),
        grid=(steps,),
        in_specs=[
            pl.BlockSpec((rows, block), lambda k: (0, offset * steps + k)),
            pl.BlockSpec((None, units, block), lambda k: (0, 0, k)),
            tile,
            tile,
        ]
        + [ANY] * len(after),
        out_specs=[tile] * 2,
        out_shape=[jax.ShapeDtypeStruct((rows, units), jnp.bfloat16)] * 2,
        scratch_shapes=[pltpu.VMEM((rows, units), jnp.float32)],
        compiler_params=params(24),
        cost_estimate=takes(micros),
        name="hidden_grad",
    )(in_hbm(buf), in_vmem(w_down), for_gate, for_up, *after)


def weight_part(kind, buf, base, width, other, place, own, received=None, after=(), micros=LONG):
    rows = buf.shape[0]
    units = other.shape[1]
    shape = (width, units) if kind == "rows" else (units, width)
    half = shape[0] // 2

    def product(buf_ref, other_ref):
        if kind == "rows":
            return dot_tn(buf_ref[...], other_ref[...])
        return dot_tn(other_ref[...], buf_ref[...])

    def plain(place_ref, buf_ref, other_ref, out_ref):
        out_ref[...] = product(buf_ref, other_ref).astype(jnp.bfloat16)

    def summed(place_ref, buf_ref, other_ref, in_ref, fwd_ref, bwd_ref, keep1_ref, keep3_ref, own_ref):
        j = pl.program_id(0)
        total = product(buf_ref, other_ref) + in_ref[...].astype(jnp.float32)
        total = total.astype(jnp.bfloat16)
        low, high = total[:half], total[half:]

        @pl.when(j == 0)
        def _():
            fwd_ref[0] = low
            bwd_ref[0] = high

        @pl.when(j == 1)
        def _():
            keep1_ref[...] = low
            fwd_ref[1] = high

        @pl.when(j == 2)
        def _():
            own_ref[...] = total

        @pl.when(j == 3)
        def _():
            bwd_ref[1] = low
            keep3_ref[...] = high

    def column(j, at):
        z, core = at[0] // 2, at[0] % 2
        wanted = core if own else 1 - core
        return (0, base + (z + 6 - j) % 4 * 2 + wanted)

    ins = [
        pl.BlockSpec((rows, width), column),
        pl.BlockSpec((rows, units), lambda j, at: (0, 0)),
    ]
    flat = jnp.bfloat16
    if received is None:
        outs = pl.BlockSpec((None,) + shape, lambda j, at: (j, 0, 0))
        out_shape = jax.ShapeDtypeStruct((4,) + shape, flat)
        args = (in_hbm(buf), other)
    else:
        ins.append(pl.BlockSpec((None,) + shape, lambda j, at: (j, 0, 0)))
        shapes = [(2, half, shape[1])] * 2 + [(half, shape[1])] * 2 + [shape]
        outs = [pl.BlockSpec(s, lambda j, at, n=len(s): (0,) * n) for s in shapes]
        out_shape = [jax.ShapeDtypeStruct(s, flat) for s in shapes]
        args = (in_hbm(buf), other, received)
    ins += [ANY] * len(after)
    body = plain if received is None else summed
    return pl.pallas_call(
        ordered(body, 1 + len(args), len(after)),
        grid_spec=pltpu.PrefetchScalarGridSpec(
            num_scalar_prefetch=1, grid=(4,), in_specs=ins, out_specs=outs
        ),
        out_shape=out_shape,
        compiler_params=params(18),
        cost_estimate=takes(micros),
        name="weight_part",
    )(place, *args, *after)


def input_rows(d_gate, d_up, w_gate, w_up, after=(), micros=LONG):
    rows, units = d_gate.shape
    width = w_gate.shape[1]
    block = 512

    def body(dg_ref, du_ref, wg_ref, wu_ref, out_ref):
        total = dot_nt(dg_ref[...], wg_ref[...]) + dot_nt(du_ref[...], wu_ref[...])
        out_ref[...] = total.astype(jnp.bfloat16)

    whole = pl.BlockSpec((rows, units), lambda j: (0, 0))
    weight = pl.BlockSpec((None, block, units), lambda j: (0, j, 0))
    return pl.pallas_call(
        ordered(body, 4, len(after)),
        grid=(width // block,),
        in_specs=[whole, whole, weight, weight] + [ANY] * len(after),
        out_specs=pl.BlockSpec((rows, block), lambda j: (0, j)),
        out_shape=pltpu.HBM((rows, width), jnp.bfloat16),
        compiler_params=params(16),
        cost_estimate=takes(micros),
        name="input_rows",
    )(d_gate, d_up, in_vmem(w_gate), in_vmem(w_up), *after)


def passed_on(parts, hop, after=(), micros=LONG):
    half, width = parts[2].shape

    def body(up_ref, down_ref, low_ref, high_ref, fwd_ref, bwd_ref):
        fwd = up_ref[...].astype(jnp.float32) + low_ref[...].astype(jnp.float32)
        bwd = down_ref[...].astype(jnp.float32) + high_ref[...].astype(jnp.float32)
        fwd_ref[...] = fwd.astype(jnp.bfloat16)
        bwd_ref[...] = bwd.astype(jnp.bfloat16)

    block = half // 2
    flat = pl.BlockSpec((block, width), lambda j: (j, 0))
    first = pl.BlockSpec((None, block, width), lambda j: (0, j, 0))
    return pl.pallas_call(
        ordered(body, 4, len(after)),
        grid=(2,),
        in_specs=[flat, flat, first, first] + [ANY] * len(after),
        out_specs=[flat, flat],
        out_shape=[jax.ShapeDtypeStruct((half, width), jnp.bfloat16)] * 2,
        compiler_params=params(8),
        cost_estimate=takes(micros),
        name="passed_on",
    )(parts[2], parts[3], *hop, *after)


def finished(parts, hop, last, after=(), micros=LONG):
    half, width = parts[2].shape

    def body(own_ref, ahead_ref, behind_ref, low_ref, high_ref, out_ref):
        own = own_ref[...].astype(jnp.float32)

        def store(near_ref, far_ref):
            total = own + near_ref[...].astype(jnp.float32) + far_ref[...].astype(jnp.float32)
            out_ref[...] = (total * weight_factor).astype(jnp.bfloat16)

        @pl.when(pl.program_id(0) == 0)
        def _():
            store(ahead_ref, low_ref)

        @pl.when(pl.program_id(0) == 1)
        def _():
            store(behind_ref, high_ref)

    tile = pl.BlockSpec((half, width), lambda j: (j, 0))
    second = pl.BlockSpec((None, half, width), lambda j: (1, 0, 0))
    whole = pl.BlockSpec((half, width), lambda j: (0, 0))
    return pl.pallas_call(
        ordered(body, 5, len(after)),
        grid=(2,),
        in_specs=[tile, second, second, whole, whole] + [ANY] * len(after),
        out_specs=tile,
        out_shape=jax.ShapeDtypeStruct((2 * half, width), jnp.bfloat16),
        compiler_params=params(10),
        cost_estimate=takes(micros),
        name="finished",
    )(parts[4], hop[1], hop[0], *last, *after)


def combine(select, returned, after=()):
    slots, tok = select.shape
    width = returned.shape[1]
    block = 1024

    def body(sel_ref, in_ref, out_ref):
        out_ref[...] = dot_tn(sel_ref[...], in_ref[...]).astype(jnp.bfloat16)

    return pl.pallas_call(
        ordered(body, 2, len(after)),
        grid=(width // block,),
        in_specs=[
            pl.BlockSpec((slots, tok), lambda j: (0, 0)),
            pl.BlockSpec((slots, block), lambda j: (0, j)),
        ]
        + [ANY] * len(after),
        out_specs=pl.BlockSpec((tok, block), lambda j: (0, j)),
        out_shape=jax.ShapeDtypeStruct((tok, width), jnp.bfloat16),
        compiler_params=params(12),
        cost_estimate=takes(5),
        name="combine",
    )(select, in_hbm(returned), *after)


def shards(tokens_in, out_grad, expert_ids, router_codes, amax_history, w_gate, w_up, w_down):
    n_dp = lax.axis_size("dp")
    peers = lax.axis_size("expert")
    width = tokens_in.shape[1]
    experts = amax_history.shape[0]
    part = width // n_dp
    place = lax.axis_index("dp").astype(jnp.int32).reshape(1)

    swap = [(i, i ^ 1) for i in range(n_dp)]
    ahead = [(i, (i + 2) % n_dp) for i in range(n_dp)]
    behind = [(i, (i - 2) % n_dp) for i in range(n_dp)]

    def exchange(buf):
        blocks = buf.reshape(peers, -1, buf.shape[1])
        out = lax.all_to_all(blocks, "expert", split_axis=0, concat_axis=0, tiled=True)
        return out.reshape(buf.shape)

    def corner(value):
        return value[:16, :128] * 2

    def swapped(value):
        return lax.ppermute(value, "dp", swap)

    def one_hop(fwd, bwd):
        return lax.ppermute(fwd, "dp", ahead), lax.ppermute(bwd, "dp", behind)

    sent, select = pack(
        tokens_in, out_grad, expert_ids.T, router_codes.T, amax_history.T, place
    )
    rows = exchange(sent)
    hidden, for_gate, for_up = forward(rows, w_gate, w_up)
    down = ("columns", rows, width // part, part, hidden)
    other_down = weight_part(*down, place, False, micros=MICROS['oD'])
    d_gate, d_up = hidden_grad(rows, 1, w_down, for_gate, for_up, after=(other_down,), micros=MICROS['hg'])
    own_down = weight_part(*down, place, True, swapped(other_down), after=(d_gate,), micros=MICROS['wD'])
    hop_down = one_hop(*own_down[:2])
    gate = ("rows", rows, 0, part, d_gate)
    other_gate = weight_part(
        *gate, place, False, after=tuple(own_down), micros=MICROS["oG"]
    )
    rows_back = input_rows(
        d_gate, d_up, w_gate, w_up, after=(other_gate,), micros=MICROS["i0"]
    )
    back = exchange(rows_back)
    next_down = passed_on(
        own_down, hop_down, after=(corner(rows_back),), micros=MICROS["nD"]
    )
    last_down = one_hop(*next_down)
    own_gate = weight_part(
        *gate, place, True, swapped(other_gate), after=next_down, micros=MICROS["wG"]
    )
    up = ("rows", rows, 0, part, d_up)
    other_up = weight_part(*up, place, False, after=tuple(own_gate), micros=MICROS["oU"])
    hop_gate = one_hop(*own_gate[:2])
    grad_down = finished(own_down, hop_down, last_down, after=(other_up,), micros=MICROS["fD"])
    own_up = weight_part(
        *up, place, True, swapped(other_up), after=(grad_down,), micros=MICROS["wU"]
    )
    hop_up = one_hop(*own_up[:2])
    next_gate = passed_on(own_gate, hop_gate, after=own_up[:2], micros=MICROS["nG"])
    last_gate = one_hop(*next_gate)
    next_up = passed_on(own_up, hop_up, after=next_gate, micros=MICROS["nU"])
    last_up = one_hop(*next_up)
    grad_tokens = combine(select, back, after=next_up)
    grad_gate = finished(own_gate, hop_gate, last_gate, after=(grad_tokens,), micros=MICROS["fG"])
    grad_up = finished(own_up, hop_up, last_up, after=(grad_gate,), micros=MICROS["fU"])
    return (grad_tokens, grad_gate[None], grad_up[None], grad_down[None])


def solution(mesh):
    return jax.shard_map(
        shards,
        mesh=mesh,
        in_specs=(
            P(("dp", "expert"), None),
            P(("dp", "expert"), None),
            P(("dp", "expert"), None),
            P(("dp", "expert"), None),
            P(),
            P("expert", None, None),
            P("expert", None, None),
            P("expert", None, None),
        ),
        out_specs=(
            P(("dp", "expert"), None),
            P("expert", "dp", None),
            P("expert", "dp", None),
            P("expert", None, "dp"),
        ),
        check_vma=False,
    )
```

```python
import jax
import jax.numpy as jnp
from jax import lax
from jax.experimental import pallas as pl
from jax.experimental.pallas import tpu as pltpu
from jax.sharding import PartitionSpec as P

saturation = 2.0
weight_factor = 1.0 / 64.0
MIB = 1024 * 1024


def params(limit):
    return pltpu.CompilerParams(vmem_limit_bytes=limit * MIB)


def cost(flops, nbytes):
    return pl.CostEstimate(flops=int(flops), bytes_accessed=int(nbytes), transcendentals=0)


def dot_nn(a, b):
    return lax.dot_general(a, b, (((1,), (0,)), ((), ())), preferred_element_type=jnp.float32)


def dot_nt(a, b):
    return lax.dot_general(a, b, (((1,), (1,)), ((), ())), preferred_element_type=jnp.float32)


def dot_tn(a, b):
    return lax.dot_general(a, b, (((0,), (0,)), ((), ())), preferred_element_type=jnp.float32)


ANY = pl.BlockSpec(memory_space=pl.ANY)


LONG = 1000
MICROS = {'oD': 5, 'hg': 5, 'wD': 5, 'i0': 100, 'oG': 100, 'nD': 100, 'oU': 100, 'wG': 100, 'wU': 100, 'nG': 100, 'fD': 100, 'nU': 100, 'fG': 100, 'fU': 100}


def takes(micros):
    return cost(micros * 1.15e9, 1e6)


def in_hbm(value):
    return pltpu.with_memory_space_constraint(value, pltpu.HBM)


def ordered(body, n_read, n_after):
    if n_after == 0:
        return body
    return lambda *refs: body(*refs[:n_read], *refs[n_read + n_after :])


def in_vmem(value):
    return pltpu.with_memory_space_constraint(value, pltpu.VMEM)


def pack(tokens, grad, ids, codes, history, place):
    tok, width = tokens.shape
    experts = history.shape[1]
    cap = tok * 2 * 2 // experts
    slots = experts * cap
    step = 2048
    nx = width // step

    def body(ids_ref, codes_ref, hist_ref, x_ref, g_ref, out_ref, sel_ref, fac_ref):
        j = pl.program_id(0)

        @pl.when(j == 0)
        def _():
            rows = lax.broadcasted_iota(jnp.int32, (tok, tok), 0)
            cols = lax.broadcasted_iota(jnp.int32, (tok, tok), 1)
            earlier = (rows < cols).astype(jnp.bfloat16)
            expert = lax.broadcasted_iota(jnp.int32, (experts, tok), 0)
            largest = jnp.max(hist_ref[...], axis=0, keepdims=True).astype(jnp.float32)
            diagonal = lax.broadcasted_iota(
                jnp.int32, (experts, experts), 0
            ) == lax.broadcasted_iota(jnp.int32, (experts, experts), 1)
            wide = jnp.broadcast_to(largest, (experts, experts))
            magnitude = jnp.sum(jnp.where(diagonal, wide, 0.0), axis=1, keepdims=True)
            scale = jnp.zeros((experts, 1), jnp.float32)
            inverse = jnp.zeros((experts, 1), jnp.float32)
            for value in range(-2, 3):
                scale = jnp.where(magnitude == value, 2.0**-value, scale)
                inverse = jnp.where(magnitude == value, 2.0**value, inverse)
            id_rows = [ids_ref[k : k + 1, :] for k in range(2)]
            marks = [expert == row for row in id_rows]
            count = (marks[0] | marks[1]).astype(jnp.float32)
            before = dot_nn(count.astype(jnp.bfloat16), earlier)
            slot = lax.broadcasted_iota(jnp.int32, (slots, tok), 0)
            select = jnp.zeros((slots, tok), jnp.float32)
            factor = jnp.zeros((slots, tok), jnp.float32)
            unscale = jnp.zeros((slots, tok), jnp.float32)
            for k in range(2):
                place = jnp.sum(jnp.where(marks[k], before, 0.0), axis=0, keepdims=True)
                dest = id_rows[k] * cap + place.astype(jnp.int32)
                chosen = jnp.sum(jnp.where(marks[k], scale, 0.0), axis=0, keepdims=True)
                back = jnp.sum(jnp.where(marks[k], inverse, 0.0), axis=0, keepdims=True)
                weight = codes_ref[k : k + 1, :].astype(jnp.float32) / 64.0 * chosen
                hit = slot == dest
                select = jnp.where(hit, 1.0, select)
                factor = jnp.where(hit, weight, factor)
                unscale = jnp.where(hit, back, unscale)
            sel_ref[...] = select.astype(jnp.bfloat16)
            fac_ref[0] = jnp.sum(factor, axis=1, keepdims=True)
            fac_ref[1] = jnp.sum(unscale, axis=1, keepdims=True)

        @pl.when(j < nx)
        def _():
            out_ref[...] = dot_nn(sel_ref[...], x_ref[...]).astype(jnp.bfloat16)

        @pl.when(j >= nx)
        def _():
            picked = dot_nn(sel_ref[...], g_ref[...])
            clipped = jnp.clip(picked * fac_ref[0], -saturation, saturation)
            rounded = clipped.astype(jnp.bfloat16).astype(jnp.float32)
            out_ref[...] = (rounded * fac_ref[1]).astype(jnp.bfloat16)

    whole = lambda shape: pl.BlockSpec(shape, lambda j: (0,) * len(shape))
    return pl.pallas_call(
        ordered(body, 5, 1),
        grid=(2 * nx,),
        in_specs=[
            whole(ids.shape),
            whole(codes.shape),
            whole(history.shape),
            pl.BlockSpec((tok, step), lambda j: (0, jnp.minimum(j, nx - 1))),
            pl.BlockSpec((tok, step), lambda j: (0, jnp.maximum(j - nx, 0))),
            ANY,
        ],
        out_specs=[pl.BlockSpec((slots, step), lambda j: (0, j)), whole((slots, tok))],
        out_shape=[
            pltpu.VMEM((slots, 2 * width), jnp.bfloat16),
            jax.ShapeDtypeStruct((slots, tok), jnp.bfloat16),
        ],
        scratch_shapes=[pltpu.VMEM((2, slots, 1), jnp.float32)],
        compiler_params=params(22),
        cost_estimate=takes(10),
        name="pack",
    )(in_hbm(ids), in_hbm(codes), in_hbm(history), in_hbm(tokens), in_hbm(grad), place)


def forward(first, w_gate, w_up, place):
    rows = first.shape[0]
    width, units = w_gate.shape[1:]
    block = 1024
    steps = width // block
    part = width // 8

    def body(place_ref, x_ref, q_ref, wg_ref, wu_ref, hidden_ref, for_gate_ref, for_up_ref, down_ref):
        k = pl.program_id(0)

        @pl.when(k == 0)
        def _():
            for_up_ref[...] = dot_nn(x_ref[...], wg_ref[...])
            for_gate_ref[...] = dot_nn(x_ref[...], wu_ref[...])

        @pl.when((k > 0) & (k < steps - 1))
        def _():
            for_up_ref[...] += dot_nn(x_ref[...], wg_ref[...])
            for_gate_ref[...] += dot_nn(x_ref[...], wu_ref[...])

        @pl.when(k == steps - 1)
        def _():
            gate = for_up_ref[...] + dot_nn(x_ref[...], wg_ref[...])
            up = for_gate_ref[...] + dot_nn(x_ref[...], wu_ref[...])
            sig = jax.nn.sigmoid(gate)
            act = gate * sig
            hidden_ref[...] = (act * up).astype(jnp.bfloat16)
            for_gate_ref[...] = up * sig * (1.0 + gate * (1.0 - sig))
            for_up_ref[...] = act

        @pl.when(k >= steps)
        def _():
            down_ref[...] = dot_tn(hidden_ref[...], q_ref[...]).astype(jnp.bfloat16)

    def column(k, at):
        z, core = at[0] // 2, at[0] % 2
        j = jnp.maximum(k - steps, 0)
        return (0, width // part + (z + 6 - j) % 4 * 2 + 1 - core)

    held = lambda k: jnp.minimum(k, steps - 1)
    out = pl.BlockSpec((rows, units), lambda k, at: (0, 0))
    weight = pl.BlockSpec((None, block, units), lambda k, at: (0, held(k), 0))
    return pl.pallas_call(
        body,
        grid_spec=pltpu.PrefetchScalarGridSpec(
            num_scalar_prefetch=1,
            grid=(steps + 4,),
            in_specs=[
                pl.BlockSpec((rows, block), lambda k, at: (0, held(k))),
                pl.BlockSpec((rows, part), column),
                weight,
                weight,
            ],
            out_specs=[
                out,
                out,
                out,
                pl.BlockSpec((None, units, part), lambda k, at: (jnp.maximum(k - steps, 0), 0, 0)),
            ],
        ),
        out_shape=[
            jax.ShapeDtypeStruct((rows, units), jnp.bfloat16),
            jax.ShapeDtypeStruct((rows, units), jnp.float32),
            jax.ShapeDtypeStruct((rows, units), jnp.float32),
            jax.ShapeDtypeStruct((4, units, part), jnp.bfloat16),
        ],
        compiler_params=params(26),
        cost_estimate=takes(10),
        name="forward",
    )(place, in_hbm(first), in_hbm(first), in_vmem(w_gate), in_vmem(w_up))


def hidden_grad(buf, offset, w_down, for_gate, for_up, after=(), micros=LONG):
    rows = buf.shape[0]
    units, width = w_down.shape[1:]
    block = 1024
    steps = width // block

    def body(q_ref, wd_ref, for_gate_ref, for_up_ref, d_gate_ref, d_up_ref, sum_ref):
        k = pl.program_id(0)
        part = dot_nt(q_ref[...], wd_ref[...])

        @pl.when(k == 0)
        def _():
            sum_ref[...] = part

        @pl.when((k > 0) & (k < steps - 1))
        def _():
            sum_ref[...] += part

        @pl.when(k == steps - 1)
        def _():
            total = sum_ref[...] + part
            d_gate_ref[...] = (total * for_gate_ref[...]).astype(jnp.bfloat16)
            d_up_ref[...] = (total * for_up_ref[...]).astype(jnp.bfloat16)

    tile = pl.BlockSpec((rows, units), lambda k: (0, 0))
    return pl.pallas_call(
        ordered(body, 4, len(after)),
        grid=(steps,),
        in_specs=[
            pl.BlockSpec((rows, block), lambda k: (0, offset * steps + k)),
            pl.BlockSpec((None, units, block), lambda k: (0, 0, k)),
            tile,
            tile,
        ]
        + [ANY] * len(after),
        out_specs=[tile] * 2,
        out_shape=[jax.ShapeDtypeStruct((rows, units), jnp.bfloat16)] * 2,
        scratch_shapes=[pltpu.VMEM((rows, units), jnp.float32)],
        compiler_params=params(24),
        cost_estimate=takes(micros),
        name="hidden_grad",
    )(in_hbm(buf), in_vmem(w_down), for_gate, for_up, *after)


def weight_part(kind, buf, base, width, other, place, own, received=None, after=(), micros=LONG):
    rows = buf.shape[0]
    units = other.shape[1]
    shape = (width, units) if kind == "rows" else (units, width)
    half = shape[0] // 2

    def product(buf_ref, other_ref):
        if kind == "rows":
            return dot_tn(buf_ref[...], other_ref[...])
        return dot_tn(other_ref[...], buf_ref[...])

    def plain(place_ref, buf_ref, other_ref, out_ref):
        out_ref[...] = product(buf_ref, other_ref).astype(jnp.bfloat16)

    def summed(place_ref, buf_ref, other_ref, in_ref, fwd_ref, bwd_ref, keep1_ref, keep3_ref, own_ref):
        j = pl.program_id(0)
        total = product(buf_ref, other_ref) + in_ref[...].astype(jnp.float32)
        total = total.astype(jnp.bfloat16)
        low, high = total[:half], total[half:]

        @pl.when(j == 0)
        def _():
            fwd_ref[0] = low
            bwd_ref[0] = high

        @pl.when(j == 1)
        def _():
            keep1_ref[...] = low
            fwd_ref[1] = high

        @pl.when(j == 2)
        def _():
            own_ref[...] = total

        @pl.when(j == 3)
        def _():
            bwd_ref[1] = low
            keep3_ref[...] = high

    def column(j, at):
        z, core = at[0] // 2, at[0] % 2
        wanted = core if own else 1 - core
        return (0, base + (z + 6 - j) % 4 * 2 + wanted)

    ins = [
        pl.BlockSpec((rows, width), column),
        pl.BlockSpec((rows, units), lambda j, at: (0, 0)),
    ]
    flat = jnp.bfloat16
    if received is None:
        outs = pl.BlockSpec((None,) + shape, lambda j, at: (j, 0, 0))
        out_shape = jax.ShapeDtypeStruct((4,) + shape, flat)
        args = (in_hbm(buf), other)
    else:
        ins.append(pl.BlockSpec((None,) + shape, lambda j, at: (j, 0, 0)))
        shapes = [(2, half, shape[1])] * 2 + [(half, shape[1])] * 2 + [shape]
        outs = [pl.BlockSpec(s, lambda j, at, n=len(s): (0,) * n) for s in shapes]
        out_shape = [jax.ShapeDtypeStruct(s, flat) for s in shapes[:2]]
        out_shape += [pltpu.HBM(s, flat) for s in shapes[2:]]
        args = (in_hbm(buf), other, received)
    ins += [ANY] * len(after)
    body = plain if received is None else summed
    return pl.pallas_call(
        ordered(body, 1 + len(args), len(after)),
        grid_spec=pltpu.PrefetchScalarGridSpec(
            num_scalar_prefetch=1, grid=(4,), in_specs=ins, out_specs=outs
        ),
        out_shape=out_shape,
        compiler_params=params(18),
        cost_estimate=takes(micros),
        name="weight_part",
    )(place, *args, *after)


def input_rows(d_gate, d_up, w_gate, w_up, after=(), micros=LONG):
    rows, units = d_gate.shape
    width = w_gate.shape[1]
    block = 512

    def body(dg_ref, du_ref, wg_ref, wu_ref, out_ref):
        total = dot_nt(dg_ref[...], wg_ref[...]) + dot_nt(du_ref[...], wu_ref[...])
        out_ref[...] = total.astype(jnp.bfloat16)

    whole = pl.BlockSpec((rows, units), lambda j: (0, 0))
    weight = pl.BlockSpec((None, block, units), lambda j: (0, j, 0))
    return pl.pallas_call(
        ordered(body, 4, len(after)),
        grid=(width // block,),
        in_specs=[whole, whole, weight, weight] + [ANY] * len(after),
        out_specs=pl.BlockSpec((rows, block), lambda j: (0, j)),
        out_shape=pltpu.HBM((rows, width), jnp.bfloat16),
        compiler_params=params(16),
        cost_estimate=takes(micros),
        name="input_rows",
    )(d_gate, d_up, in_vmem(w_gate), in_vmem(w_up), *after)


def passed_on(parts, hop, after=(), micros=LONG):
    half, width = parts[2].shape

    def body(up_ref, down_ref, low_ref, high_ref, fwd_ref, bwd_ref):
        fwd = up_ref[...].astype(jnp.float32) + low_ref[...].astype(jnp.float32)
        bwd = down_ref[...].astype(jnp.float32) + high_ref[...].astype(jnp.float32)
        fwd_ref[...] = fwd.astype(jnp.bfloat16)
        bwd_ref[...] = bwd.astype(jnp.bfloat16)

    block = half // 2
    flat = pl.BlockSpec((block, width), lambda j: (j, 0))
    first = pl.BlockSpec((None, block, width), lambda j: (0, j, 0))
    return pl.pallas_call(
        ordered(body, 4, len(after)),
        grid=(2,),
        in_specs=[flat, flat, first, first] + [ANY] * len(after),
        out_specs=[flat, flat],
        out_shape=[jax.ShapeDtypeStruct((half, width), jnp.bfloat16)] * 2,
        compiler_params=params(8),
        cost_estimate=takes(micros),
        name="passed_on",
    )(in_hbm(parts[2]), in_hbm(parts[3]), *hop, *after)


def finished(parts, hop, last, after=(), micros=LONG):
    half, width = parts[2].shape

    def body(own_ref, ahead_ref, behind_ref, low_ref, high_ref, out_ref):
        own = own_ref[...].astype(jnp.float32)

        def store(near_ref, far_ref):
            total = own + near_ref[...].astype(jnp.float32) + far_ref[...].astype(jnp.float32)
            out_ref[...] = (total * weight_factor).astype(jnp.bfloat16)

        @pl.when(pl.program_id(0) == 0)
        def _():
            store(ahead_ref, low_ref)

        @pl.when(pl.program_id(0) == 1)
        def _():
            store(behind_ref, high_ref)

    tile = pl.BlockSpec((half, width), lambda j: (j, 0))
    second = pl.BlockSpec((None, half, width), lambda j: (1, 0, 0))
    whole = pl.BlockSpec((half, width), lambda j: (0, 0))
    return pl.pallas_call(
        ordered(body, 5, len(after)),
        grid=(2,),
        in_specs=[tile, second, second, whole, whole] + [ANY] * len(after),
        out_specs=tile,
        out_shape=jax.ShapeDtypeStruct((2 * half, width), jnp.bfloat16),
        compiler_params=params(10),
        cost_estimate=takes(micros),
        name="finished",
    )(in_hbm(parts[4]), hop[1], hop[0], *last, *after)


def combine(select, returned, after=()):
    slots, tok = select.shape
    width = returned.shape[1]
    block = 1024

    def body(sel_ref, in_ref, out_ref):
        out_ref[...] = dot_tn(sel_ref[...], in_ref[...]).astype(jnp.bfloat16)

    return pl.pallas_call(
        ordered(body, 2, len(after)),
        grid=(width // block,),
        in_specs=[
            pl.BlockSpec((slots, tok), lambda j: (0, 0)),
            pl.BlockSpec((slots, block), lambda j: (0, j)),
        ]
        + [ANY] * len(after),
        out_specs=pl.BlockSpec((tok, block), lambda j: (0, j)),
        out_shape=jax.ShapeDtypeStruct((tok, width), jnp.bfloat16),
        compiler_params=params(12),
        cost_estimate=takes(5),
        name="combine",
    )(in_hbm(select), in_hbm(returned), *after)


def shards(tokens_in, out_grad, expert_ids, router_codes, amax_history, w_gate, w_up, w_down):
    n_dp = lax.axis_size("dp")
    peers = lax.axis_size("expert")
    width = tokens_in.shape[1]
    experts = amax_history.shape[0]
    part = width // n_dp
    place = lax.axis_index("dp").astype(jnp.int32).reshape(1)

    swap = [(i, i ^ 1) for i in range(n_dp)]
    ahead = [(i, (i + 2) % n_dp) for i in range(n_dp)]
    behind = [(i, (i - 2) % n_dp) for i in range(n_dp)]

    def exchange(buf):
        blocks = buf.reshape(peers, -1, buf.shape[1])
        out = lax.all_to_all(blocks, "expert", split_axis=0, concat_axis=0, tiled=True)
        return out.reshape(buf.shape)

    def corner(value):
        return value[:16, :128] * 2

    def named(parts):
        return (*parts[:2], *[in_hbm(value) for value in parts[2:]])

    def swapped(value):
        return lax.ppermute(value, "dp", swap)

    def one_hop(fwd, bwd):
        return lax.ppermute(fwd, "dp", ahead), lax.ppermute(bwd, "dp", behind)

    sent, select = pack(
        tokens_in, out_grad, expert_ids.T, router_codes.T, amax_history.T, place
    )
    rows = exchange(sent)
    hidden, for_gate, for_up, other_down = forward(rows, w_gate, w_up, place)
    down = ("columns", rows, width // part, part, hidden)
    d_gate, d_up = hidden_grad(rows, 1, w_down, for_gate, for_up, after=(other_down,), micros=MICROS['hg'])
    own_down = weight_part(*down, place, True, swapped(other_down), after=(d_gate,), micros=MICROS['wD'])
    hop_down = one_hop(*own_down[:2])
    gate = ("rows", rows, 0, part, d_gate)
    other_gate = weight_part(
        *gate, place, False, after=named(own_down), micros=MICROS["oG"]
    )
    rows_back = input_rows(
        d_gate, d_up, w_gate, w_up, after=(other_gate,), micros=MICROS["i0"]
    )
    back = exchange(rows_back)
    next_down = passed_on(
        own_down, hop_down, after=(corner(rows_back),), micros=MICROS["nD"]
    )
    last_down = one_hop(*next_down)
    own_gate = weight_part(
        *gate, place, True, swapped(other_gate), after=next_down, micros=MICROS["wG"]
    )
    up = ("rows", rows, 0, part, d_up)
    other_up = weight_part(*up, place, False, after=named(own_gate), micros=MICROS["oU"])
    hop_gate = one_hop(*own_gate[:2])
    grad_down = finished(own_down, hop_down, last_down, after=(other_up,), micros=MICROS["fD"])
    own_up = weight_part(
        *up, place, True, swapped(other_up), after=(in_hbm(grad_down),), micros=MICROS["wU"]
    )
    hop_up = one_hop(*own_up[:2])
    next_gate = passed_on(own_gate, hop_gate, after=own_up[:2], micros=MICROS["nG"])
    last_gate = one_hop(*next_gate)
    next_up = passed_on(own_up, hop_up, after=next_gate, micros=MICROS["nU"])
    last_up = one_hop(*next_up)
    grad_tokens = combine(select, back, after=next_up)
    grad_gate = finished(own_gate, hop_gate, last_gate, after=(in_hbm(grad_tokens),), micros=MICROS["fG"])
    grad_up = finished(own_up, hop_up, last_up, after=(in_hbm(grad_gate),), micros=MICROS["fU"])
    return (grad_tokens, grad_gate[None], grad_up[None], grad_down[None])


def solution(mesh):
    return jax.shard_map(
        shards,
        mesh=mesh,
        in_specs=(
            P(("dp", "expert"), None),
            P(("dp", "expert"), None),
            P(("dp", "expert"), None),
            P(("dp", "expert"), None),
            P(),
            P("expert", None, None),
            P("expert", None, None),
            P("expert", None, None),
        ),
        out_specs=(
            P(("dp", "expert"), None),
            P("expert", "dp", None),
            P("expert", "dp", None),
            P("expert", None, "dp"),
        ),
        check_vma=False,
    )
```

```python
import jax
import jax.numpy as jnp
from jax import lax
from jax.experimental import pallas as pl
from jax.experimental.pallas import tpu as pltpu
from jax.sharding import PartitionSpec as P

saturation = 2.0
weight_factor = 1.0 / 64.0
MIB = 1024 * 1024


def params(limit):
    return pltpu.CompilerParams(vmem_limit_bytes=limit * MIB)


def cost(flops, nbytes):
    return pl.CostEstimate(flops=int(flops), bytes_accessed=int(nbytes), transcendentals=0)


def dot_nn(a, b):
    return lax.dot_general(a, b, (((1,), (0,)), ((), ())), preferred_element_type=jnp.float32)


def dot_nt(a, b):
    return lax.dot_general(a, b, (((1,), (1,)), ((), ())), preferred_element_type=jnp.float32)


def dot_tn(a, b):
    return lax.dot_general(a, b, (((0,), (0,)), ((), ())), preferred_element_type=jnp.float32)


ANY = pl.BlockSpec(memory_space=pl.ANY)


LONG = 1000
MICROS = {'oD': 5, 'hg': 5, 'wD': 5, 'i0': 100, 'oG': 100, 'nD': 100, 'oU': 100, 'wG': 100, 'wU': 100, 'nG': 100, 'fD': 100, 'nU': 100, 'fG': 100, 'fU': 100}


def takes(micros):
    return cost(micros * 1.15e9, 1e6)


def in_hbm(value):
    return pltpu.with_memory_space_constraint(value, pltpu.HBM)


def ordered(body, n_read, n_after):
    if n_after == 0:
        return body
    return lambda *refs: body(*refs[:n_read], *refs[n_read + n_after :])


def in_vmem(value):
    return pltpu.with_memory_space_constraint(value, pltpu.VMEM)


def pack(tokens, grad, ids, codes, history, place):
    tok, width = tokens.shape
    experts = history.shape[1]
    cap = tok * 2 * 2 // experts
    slots = experts * cap
    step = 2048
    nx = width // step

    def body(ids_ref, codes_ref, hist_ref, x_ref, g_ref, out_ref, sel_ref, fac_ref):
        j = pl.program_id(0)

        @pl.when(j == 0)
        def _():
            rows = lax.broadcasted_iota(jnp.int32, (tok, tok), 0)
            cols = lax.broadcasted_iota(jnp.int32, (tok, tok), 1)
            earlier = (rows < cols).astype(jnp.bfloat16)
            expert = lax.broadcasted_iota(jnp.int32, (experts, tok), 0)
            largest = jnp.max(hist_ref[...], axis=0, keepdims=True).astype(jnp.float32)
            diagonal = lax.broadcasted_iota(
                jnp.int32, (experts, experts), 0
            ) == lax.broadcasted_iota(jnp.int32, (experts, experts), 1)
            wide = jnp.broadcast_to(largest, (experts, experts))
            magnitude = jnp.sum(jnp.where(diagonal, wide, 0.0), axis=1, keepdims=True)
            scale = jnp.zeros((experts, 1), jnp.float32)
            inverse = jnp.zeros((experts, 1), jnp.float32)
            for value in range(-2, 3):
                scale = jnp.where(magnitude == value, 2.0**-value, scale)
                inverse = jnp.where(magnitude == value, 2.0**value, inverse)
            id_rows = [ids_ref[k : k + 1, :] for k in range(2)]
            marks = [expert == row for row in id_rows]
            count = (marks[0] | marks[1]).astype(jnp.float32)
            before = dot_nn(count.astype(jnp.bfloat16), earlier)
            slot = lax.broadcasted_iota(jnp.int32, (slots, tok), 0)
            select = jnp.zeros((slots, tok), jnp.float32)
            factor = jnp.zeros((slots, tok), jnp.float32)
            unscale = jnp.zeros((slots, tok), jnp.float32)
            for k in range(2):
                place = jnp.sum(jnp.where(marks[k], before, 0.0), axis=0, keepdims=True)
                dest = id_rows[k] * cap + place.astype(jnp.int32)
                chosen = jnp.sum(jnp.where(marks[k], scale, 0.0), axis=0, keepdims=True)
                back = jnp.sum(jnp.where(marks[k], inverse, 0.0), axis=0, keepdims=True)
                weight = codes_ref[k : k + 1, :].astype(jnp.float32) / 64.0 * chosen
                hit = slot == dest
                select = jnp.where(hit, 1.0, select)
                factor = jnp.where(hit, weight, factor)
                unscale = jnp.where(hit, back, unscale)
            sel_ref[...] = select.astype(jnp.bfloat16)
            fac_ref[0] = jnp.sum(factor, axis=1, keepdims=True)
            fac_ref[1] = jnp.sum(unscale, axis=1, keepdims=True)

        @pl.when(j < nx)
        def _():
            out_ref[...] = dot_nn(sel_ref[...], x_ref[...]).astype(jnp.bfloat16)

        @pl.when(j >= nx)
        def _():
            picked = dot_nn(sel_ref[...], g_ref[...])
            clipped = jnp.clip(picked * fac_ref[0], -saturation, saturation)
            rounded = clipped.astype(jnp.bfloat16).astype(jnp.float32)
            out_ref[...] = (rounded * fac_ref[1]).astype(jnp.bfloat16)

    whole = lambda shape: pl.BlockSpec(shape, lambda j: (0,) * len(shape))
    return pl.pallas_call(
        ordered(body, 5, 1),
        grid=(2 * nx,),
        in_specs=[
            whole(ids.shape),
            whole(codes.shape),
            whole(history.shape),
            pl.BlockSpec((tok, step), lambda j: (0, jnp.minimum(j, nx - 1))),
            pl.BlockSpec((tok, step), lambda j: (0, jnp.maximum(j - nx, 0))),
            ANY,
        ],
        out_specs=[pl.BlockSpec((slots, step), lambda j: (0, j)), whole((slots, tok))],
        out_shape=[
            pltpu.VMEM((slots, 2 * width), jnp.bfloat16),
            jax.ShapeDtypeStruct((slots, tok), jnp.bfloat16),
        ],
        scratch_shapes=[pltpu.VMEM((2, slots, 1), jnp.float32)],
        compiler_params=params(22),
        cost_estimate=takes(10),
        name="pack",
    )(in_hbm(ids), in_hbm(codes), in_hbm(history), in_hbm(tokens), in_hbm(grad), place)


def forward(first, w_gate, w_up, place):
    rows = first.shape[0]
    width, units = w_gate.shape[1:]
    block = 1024
    steps = width // block
    part = width // 8

    def body(place_ref, x_ref, q_ref, wg_ref, wu_ref, hidden_ref, for_gate_ref, for_up_ref, down_ref):
        k = pl.program_id(0)

        @pl.when(k == 0)
        def _():
            for_up_ref[...] = dot_nn(x_ref[...], wg_ref[...])
            for_gate_ref[...] = dot_nn(x_ref[...], wu_ref[...])

        @pl.when((k > 0) & (k < steps - 1))
        def _():
            for_up_ref[...] += dot_nn(x_ref[...], wg_ref[...])
            for_gate_ref[...] += dot_nn(x_ref[...], wu_ref[...])

        @pl.when(k == steps - 1)
        def _():
            gate = for_up_ref[...] + dot_nn(x_ref[...], wg_ref[...])
            up = for_gate_ref[...] + dot_nn(x_ref[...], wu_ref[...])
            sig = jax.nn.sigmoid(gate)
            act = gate * sig
            hidden_ref[...] = (act * up).astype(jnp.bfloat16)
            for_gate_ref[...] = up * sig * (1.0 + gate * (1.0 - sig))
            for_up_ref[...] = act

        @pl.when(k >= steps)
        def _():
            down_ref[...] = dot_tn(hidden_ref[...], q_ref[...]).astype(jnp.bfloat16)

    def column(k, at):
        z, core = at[0] // 2, at[0] % 2
        j = jnp.maximum(k - steps, 0)
        return (0, width // part + (z + 6 - j) % 4 * 2 + 1 - core)

    held = lambda k: jnp.minimum(k, steps - 1)
    out = pl.BlockSpec((rows, units), lambda k, at: (0, 0))
    weight = pl.BlockSpec((None, block, units), lambda k, at: (0, held(k), 0))
    return pl.pallas_call(
        body,
        grid_spec=pltpu.PrefetchScalarGridSpec(
            num_scalar_prefetch=1,
            grid=(steps + 4,),
            in_specs=[
                pl.BlockSpec((rows, block), lambda k, at: (0, held(k))),
                pl.BlockSpec((rows, part), column),
                weight,
                weight,
            ],
            out_specs=[
                out,
                out,
                out,
                pl.BlockSpec((None, units, part), lambda k, at: (jnp.maximum(k - steps, 0), 0, 0)),
            ],
        ),
        out_shape=[
            jax.ShapeDtypeStruct((rows, units), jnp.bfloat16),
            jax.ShapeDtypeStruct((rows, units), jnp.float32),
            jax.ShapeDtypeStruct((rows, units), jnp.float32),
            jax.ShapeDtypeStruct((4, units, part), jnp.bfloat16),
        ],
        compiler_params=params(26),
        cost_estimate=takes(10),
        name="forward",
    )(place, in_hbm(first), in_hbm(first), in_vmem(w_gate), in_vmem(w_up))


def hidden_grad(buf, offset, w_down, for_gate, for_up, after=(), micros=LONG):
    rows = buf.shape[0]
    units, width = w_down.shape[1:]
    block = 1024
    steps = width // block

    def body(q_ref, wd_ref, for_gate_ref, for_up_ref, d_gate_ref, d_up_ref, sum_ref):
        k = pl.program_id(0)
        part = dot_nt(q_ref[...], wd_ref[...])

        @pl.when(k == 0)
        def _():
            sum_ref[...] = part

        @pl.when((k > 0) & (k < steps - 1))
        def _():
            sum_ref[...] += part

        @pl.when(k == steps - 1)
        def _():
            total = sum_ref[...] + part
            d_gate_ref[...] = (total * for_gate_ref[...]).astype(jnp.bfloat16)
            d_up_ref[...] = (total * for_up_ref[...]).astype(jnp.bfloat16)

    tile = pl.BlockSpec((rows, units), lambda k: (0, 0))
    return pl.pallas_call(
        ordered(body, 4, len(after)),
        grid=(steps,),
        in_specs=[
            pl.BlockSpec((rows, block), lambda k: (0, offset * steps + k)),
            pl.BlockSpec((None, units, block), lambda k: (0, 0, k)),
            tile,
            tile,
        ]
        + [ANY] * len(after),
        out_specs=[tile] * 2,
        out_shape=[jax.ShapeDtypeStruct((rows, units), jnp.bfloat16)] * 2,
        scratch_shapes=[pltpu.VMEM((rows, units), jnp.float32)],
        compiler_params=params(24),
        cost_estimate=takes(micros),
        name="hidden_grad",
    )(in_hbm(buf), in_vmem(w_down), for_gate, for_up, *after)


def weight_part(kind, buf, base, width, other, place, own, received=None, after=(), micros=LONG, stay=2):
    rows = buf.shape[0]
    units = other.shape[1]
    shape = (width, units) if kind == "rows" else (units, width)
    half = shape[0] // 2

    def product(buf_ref, other_ref):
        if kind == "rows":
            return dot_tn(buf_ref[...], other_ref[...])
        return dot_tn(other_ref[...], buf_ref[...])

    def plain(place_ref, buf_ref, other_ref, out_ref):
        out_ref[...] = product(buf_ref, other_ref).astype(jnp.bfloat16)

    def summed(place_ref, buf_ref, other_ref, in_ref, fwd_ref, bwd_ref, keep1_ref, keep3_ref, own_ref):
        j = pl.program_id(0)
        total = product(buf_ref, other_ref) + in_ref[...].astype(jnp.float32)
        total = total.astype(jnp.bfloat16)
        low, high = total[:half], total[half:]

        @pl.when(j == 0)
        def _():
            fwd_ref[...] = low
            bwd_ref[...] = high

        @pl.when(j == 1)
        def _():
            keep1_ref[...] = low
            fwd_ref[...] = high

        @pl.when(j == 2)
        def _():
            own_ref[...] = total

        @pl.when(j == 3)
        def _():
            bwd_ref[...] = low
            keep3_ref[...] = high

    def column(j, at):
        z, core = at[0] // 2, at[0] % 2
        wanted = core if own else 1 - core
        return (0, base + (z + 6 - j) % 4 * 2 + wanted)

    ins = [
        pl.BlockSpec((rows, width), column),
        pl.BlockSpec((rows, units), lambda j, at: (0, 0)),
    ]
    flat = jnp.bfloat16
    if received is None:
        outs = pl.BlockSpec((None,) + shape, lambda j, at: (j, 0, 0))
        out_shape = jax.ShapeDtypeStruct((4,) + shape, flat)
        args = (in_hbm(buf), other)
    else:
        ins.append(pl.BlockSpec((None,) + shape, lambda j, at: (j, 0, 0)))
        shapes = [(2, half, shape[1])] * 2 + [(half, shape[1])] * 2 + [shape]
        outs = [pl.BlockSpec(s, lambda j, at, n=len(s): (0,) * n) for s in shapes]
        pair = (None,) + shapes[0][1:]
        outs[0] = pl.BlockSpec(pair, lambda j, at: (jnp.minimum(j, 1), 0, 0))
        outs[1] = pl.BlockSpec(pair, lambda j, at: (j // 3, 0, 0))
        out_shape = [jax.ShapeDtypeStruct(s, flat) for s in shapes[:stay]]
        out_shape += [pltpu.HBM(s, flat) for s in shapes[stay:]]
        args = (in_hbm(buf), other, received)
    ins += [ANY] * len(after)
    body = plain if received is None else summed
    return pl.pallas_call(
        ordered(body, 1 + len(args), len(after)),
        grid_spec=pltpu.PrefetchScalarGridSpec(
            num_scalar_prefetch=1, grid=(4,), in_specs=ins, out_specs=outs
        ),
        out_shape=out_shape,
        compiler_params=params(18),
        cost_estimate=takes(micros),
        name="weight_part",
    )(place, *args, *after)


def input_rows(d_gate, d_up, w_gate, w_up, after=(), micros=LONG):
    rows, units = d_gate.shape
    width = w_gate.shape[1]
    block = 1024

    def body(dg_ref, du_ref, wg_ref, wu_ref, out_ref):
        total = dot_nt(dg_ref[...], wg_ref[...]) + dot_nt(du_ref[...], wu_ref[...])
        out_ref[...] = total.astype(jnp.bfloat16)

    whole = pl.BlockSpec((rows, units), lambda j: (0, 0))
    weight = pl.BlockSpec((None, block, units), lambda j: (0, j, 0))
    return pl.pallas_call(
        ordered(body, 4, len(after)),
        grid=(width // block,),
        in_specs=[whole, whole, weight, weight] + [ANY] * len(after),
        out_specs=pl.BlockSpec((rows, block), lambda j: (0, j)),
        out_shape=pltpu.HBM((rows, width), jnp.bfloat16),
        compiler_params=params(24),
        cost_estimate=takes(micros),
        name="input_rows",
    )(d_gate, d_up, in_vmem(w_gate), in_vmem(w_up), *after)


def passed_on(parts, hop, after=(), micros=LONG, where=in_hbm):
    half, width = parts[2].shape

    def body(up_ref, down_ref, low_ref, high_ref, fwd_ref, bwd_ref):
        fwd = up_ref[...].astype(jnp.float32) + low_ref[...].astype(jnp.float32)
        bwd = down_ref[...].astype(jnp.float32) + high_ref[...].astype(jnp.float32)
        fwd_ref[...] = fwd.astype(jnp.bfloat16)
        bwd_ref[...] = bwd.astype(jnp.bfloat16)

    block = half // 2
    flat = pl.BlockSpec((block, width), lambda j: (j, 0))
    first = pl.BlockSpec((None, block, width), lambda j: (0, j, 0))
    return pl.pallas_call(
        ordered(body, 4, len(after)),
        grid=(2,),
        in_specs=[flat, flat, first, first] + [ANY] * len(after),
        out_specs=[flat, flat],
        out_shape=[jax.ShapeDtypeStruct((half, width), jnp.bfloat16)] * 2,
        compiler_params=params(8),
        cost_estimate=takes(micros),
        name="passed_on",
    )(where(parts[2]), where(parts[3]), *hop, *after)


def finished(parts, hop, last, after=(), micros=LONG):
    half, width = parts[2].shape

    def body(own_ref, ahead_ref, behind_ref, low_ref, high_ref, out_ref):
        own = own_ref[...].astype(jnp.float32)

        def store(near_ref, far_ref):
            total = own + near_ref[...].astype(jnp.float32) + far_ref[...].astype(jnp.float32)
            out_ref[...] = (total * weight_factor).astype(jnp.bfloat16)

        @pl.when(pl.program_id(0) == 0)
        def _():
            store(ahead_ref, low_ref)

        @pl.when(pl.program_id(0) == 1)
        def _():
            store(behind_ref, high_ref)

    tile = pl.BlockSpec((half, width), lambda j: (j, 0))
    second = pl.BlockSpec((None, half, width), lambda j: (1, 0, 0))
    whole = pl.BlockSpec((half, width), lambda j: (0, 0))
    return pl.pallas_call(
        ordered(body, 5, len(after)),
        grid=(2,),
        in_specs=[tile, second, second, whole, whole] + [ANY] * len(after),
        out_specs=tile,
        out_shape=jax.ShapeDtypeStruct((2 * half, width), jnp.bfloat16),
        compiler_params=params(10),
        cost_estimate=takes(micros),
        name="finished",
    )(in_hbm(parts[4]), hop[1], hop[0], *last, *after)


def combine(select, returned, after=()):
    slots, tok = select.shape
    width = returned.shape[1]
    block = 1024

    def body(sel_ref, in_ref, out_ref):
        out_ref[...] = dot_tn(sel_ref[...], in_ref[...]).astype(jnp.bfloat16)

    return pl.pallas_call(
        ordered(body, 2, len(after)),
        grid=(width // block,),
        in_specs=[
            pl.BlockSpec((slots, tok), lambda j: (0, 0)),
            pl.BlockSpec((slots, block), lambda j: (0, j)),
        ]
        + [ANY] * len(after),
        out_specs=pl.BlockSpec((tok, block), lambda j: (0, j)),
        out_shape=jax.ShapeDtypeStruct((tok, width), jnp.bfloat16),
        compiler_params=params(12),
        cost_estimate=takes(5),
        name="combine",
    )(in_hbm(select), in_hbm(returned), *after)


def shards(tokens_in, out_grad, expert_ids, router_codes, amax_history, w_gate, w_up, w_down):
    n_dp = lax.axis_size("dp")
    peers = lax.axis_size("expert")
    width = tokens_in.shape[1]
    experts = amax_history.shape[0]
    part = width // n_dp
    place = lax.axis_index("dp").astype(jnp.int32).reshape(1)

    swap = [(i, i ^ 1) for i in range(n_dp)]
    ahead = [(i, (i + 2) % n_dp) for i in range(n_dp)]
    behind = [(i, (i - 2) % n_dp) for i in range(n_dp)]

    def exchange(buf):
        blocks = buf.reshape(peers, -1, buf.shape[1])
        out = lax.all_to_all(blocks, "expert", split_axis=0, concat_axis=0, tiled=True)
        return out.reshape(buf.shape)

    def named(parts):
        return (*parts[:2], *[in_hbm(value) for value in parts[2:]])

    def swapped(value):
        return lax.ppermute(value, "dp", swap)

    def one_hop(fwd, bwd):
        return lax.ppermute(fwd, "dp", ahead), lax.ppermute(bwd, "dp", behind)

    sent, select = pack(
        tokens_in, out_grad, expert_ids.T, router_codes.T, amax_history.T, place
    )
    rows = exchange(sent)
    hidden, for_gate, for_up, other_down = forward(rows, w_gate, w_up, place)
    down = ("columns", rows, width // part, part, hidden)
    d_gate, d_up = hidden_grad(rows, 1, w_down, for_gate, for_up, after=(other_down,), micros=MICROS['hg'])
    own_down = weight_part(*down, place, True, swapped(other_down), after=(d_gate,), micros=MICROS['wD'])
    hop_down = one_hop(*own_down[:2])
    gate = ("rows", rows, 0, part, d_gate)
    other_gate = weight_part(
        *gate, place, False, after=named(own_down), micros=MICROS["oG"]
    )
    rows_back = input_rows(
        d_gate, d_up, w_gate, w_up, after=(other_gate,), micros=MICROS["i0"]
    )
    back = exchange(rows_back)
    next_down = passed_on(
        own_down, hop_down, after=(in_hbm(rows_back),), micros=MICROS["nD"]
    )
    last_down = one_hop(*next_down)
    own_gate = weight_part(
        *gate, place, True, swapped(other_gate), after=next_down, micros=MICROS["wG"]
    )
    up = ("rows", rows, 0, part, d_up)
    other_up = weight_part(*up, place, False, after=named(own_gate), micros=MICROS["oU"])
    hop_gate = one_hop(*own_gate[:2])
    grad_down = finished(own_down, hop_down, last_down, after=(other_up,), micros=MICROS["fD"])
    own_up = weight_part(
        *up, place, True, swapped(other_up), after=(in_hbm(grad_down),), micros=MICROS["wU"], stay=4
    )
    hop_up = one_hop(*own_up[:2])
    next_gate = passed_on(own_gate, hop_gate, after=own_up[:2], micros=MICROS["nG"])
    last_gate = one_hop(*next_gate)
    next_up = passed_on(
        own_up, hop_up, after=next_gate, micros=MICROS["nU"], where=lambda value: value
    )
    last_up = one_hop(*next_up)
    grad_tokens = combine(select, back, after=next_up)
    grad_gate = finished(own_gate, hop_gate, last_gate, after=(in_hbm(grad_tokens),), micros=MICROS["fG"])
    grad_up = finished(own_up, hop_up, last_up, after=(in_hbm(grad_gate),), micros=MICROS["fU"])
    return (grad_tokens, grad_gate[None], grad_up[None], grad_down[None])


def solution(mesh):
    return jax.shard_map(
        shards,
        mesh=mesh,
        in_specs=(
            P(("dp", "expert"), None),
            P(("dp", "expert"), None),
            P(("dp", "expert"), None),
            P(("dp", "expert"), None),
            P(),
            P("expert", None, None),
            P("expert", None, None),
            P("expert", None, None),
        ),
        out_specs=(
            P(("dp", "expert"), None),
            P("expert", "dp", None),
            P("expert", "dp", None),
            P("expert", None, "dp"),
        ),
        check_vma=False,
    )
```

```python
import jax
import jax.numpy as jnp
from jax import lax
from jax.experimental import pallas as pl
from jax.experimental.pallas import tpu as pltpu
from jax.sharding import PartitionSpec as P

saturation = 2.0
weight_factor = 1.0 / 64.0
MIB = 1024 * 1024


def params(limit):
    return pltpu.CompilerParams(vmem_limit_bytes=limit * MIB)


def cost(flops, nbytes):
    return pl.CostEstimate(flops=int(flops), bytes_accessed=int(nbytes), transcendentals=0)


def dot_nn(a, b):
    return lax.dot_general(a, b, (((1,), (0,)), ((), ())), preferred_element_type=jnp.float32)


def dot_nt(a, b):
    return lax.dot_general(a, b, (((1,), (1,)), ((), ())), preferred_element_type=jnp.float32)


def dot_tn(a, b):
    return lax.dot_general(a, b, (((0,), (0,)), ((), ())), preferred_element_type=jnp.float32)


ANY = pl.BlockSpec(memory_space=pl.ANY)


LONG = 1000
MICROS = {'oD': 5, 'hg': 5, 'wD': 5, 'i0': 100, 'oG': 100, 'nD': 100, 'oU': 100, 'wG': 100, 'wU': 100, 'nG': 100, 'fD': 100, 'nU': 100, 'fG': 100, 'fU': 100}


def takes(micros):
    return cost(micros * 1.15e9, 1e6)


def in_hbm(value):
    return pltpu.with_memory_space_constraint(value, pltpu.HBM)


def ordered(body, n_read, n_after):
    if n_after == 0:
        return body
    return lambda *refs: body(*refs[:n_read], *refs[n_read + n_after :])


def in_vmem(value):
    return pltpu.with_memory_space_constraint(value, pltpu.VMEM)


def pack(tokens, grad, ids, codes, history, place):
    tok, width = tokens.shape
    experts = history.shape[1]
    cap = tok * 2 * 2 // experts
    slots = experts * cap
    step = 2048
    nx = width // step

    def body(ids_ref, codes_ref, hist_ref, x_ref, g_ref, out_ref, sel_ref, fac_ref):
        j = pl.program_id(0)

        @pl.when(j == 0)
        def _():
            rows = lax.broadcasted_iota(jnp.int32, (tok, tok), 0)
            cols = lax.broadcasted_iota(jnp.int32, (tok, tok), 1)
            earlier = (rows < cols).astype(jnp.bfloat16)
            expert = lax.broadcasted_iota(jnp.int32, (experts, tok), 0)
            largest = jnp.max(hist_ref[...], axis=0, keepdims=True).astype(jnp.float32)
            diagonal = lax.broadcasted_iota(
                jnp.int32, (experts, experts), 0
            ) == lax.broadcasted_iota(jnp.int32, (experts, experts), 1)
            wide = jnp.broadcast_to(largest, (experts, experts))
            magnitude = jnp.sum(jnp.where(diagonal, wide, 0.0), axis=1, keepdims=True)
            scale = jnp.zeros((experts, 1), jnp.float32)
            inverse = jnp.zeros((experts, 1), jnp.float32)
            for value in range(-2, 3):
                scale = jnp.where(magnitude == value, 2.0**-value, scale)
                inverse = jnp.where(magnitude == value, 2.0**value, inverse)
            id_rows = [ids_ref[k : k + 1, :] for k in range(2)]
            marks = [expert == row for row in id_rows]
            count = (marks[0] | marks[1]).astype(jnp.float32)
            before = dot_nn(count.astype(jnp.bfloat16), earlier)
            slot = lax.broadcasted_iota(jnp.int32, (slots, tok), 0)
            select = jnp.zeros((slots, tok), jnp.float32)
            factor = jnp.zeros((slots, tok), jnp.float32)
            unscale = jnp.zeros((slots, tok), jnp.float32)
            for k in range(2):
                place = jnp.sum(jnp.where(marks[k], before, 0.0), axis=0, keepdims=True)
                dest = id_rows[k] * cap + place.astype(jnp.int32)
                chosen = jnp.sum(jnp.where(marks[k], scale, 0.0), axis=0, keepdims=True)
                back = jnp.sum(jnp.where(marks[k], inverse, 0.0), axis=0, keepdims=True)
                weight = codes_ref[k : k + 1, :].astype(jnp.float32) / 64.0 * chosen
                hit = slot == dest
                select = jnp.where(hit, 1.0, select)
                factor = jnp.where(hit, weight, factor)
                unscale = jnp.where(hit, back, unscale)
            sel_ref[...] = select.astype(jnp.bfloat16)
            fac_ref[0] = jnp.sum(factor, axis=1, keepdims=True)
            fac_ref[1] = jnp.sum(unscale, axis=1, keepdims=True)

        @pl.when(j < nx)
        def _():
            out_ref[...] = dot_nn(sel_ref[...], x_ref[...]).astype(jnp.bfloat16)

        @pl.when(j >= nx)
        def _():
            picked = dot_nn(sel_ref[...], g_ref[...])
            clipped = jnp.clip(picked * fac_ref[0], -saturation, saturation)
            rounded = clipped.astype(jnp.bfloat16).astype(jnp.float32)
            out_ref[...] = (rounded * fac_ref[1]).astype(jnp.bfloat16)

    whole = lambda shape: pl.BlockSpec(shape, lambda j: (0,) * len(shape))
    return pl.pallas_call(
        ordered(body, 5, 1),
        grid=(2 * nx,),
        in_specs=[
            whole(ids.shape),
            whole(codes.shape),
            whole(history.shape),
            pl.BlockSpec((tok, step), lambda j: (0, jnp.minimum(j, nx - 1))),
            pl.BlockSpec((tok, step), lambda j: (0, jnp.maximum(j - nx, 0))),
            ANY,
        ],
        out_specs=[pl.BlockSpec((slots, step), lambda j: (0, j)), whole((slots, tok))],
        out_shape=[
            pltpu.VMEM((slots, 2 * width), jnp.bfloat16),
            jax.ShapeDtypeStruct((slots, tok), jnp.bfloat16),
        ],
        scratch_shapes=[pltpu.VMEM((2, slots, 1), jnp.float32)],
        compiler_params=params(22),
        cost_estimate=takes(10),
        name="pack",
    )(in_hbm(ids), in_hbm(codes), in_hbm(history), in_hbm(tokens), in_hbm(grad), place)


def forward(first, w_gate, w_up, place):
    rows = first.shape[0]
    width, units = w_gate.shape[1:]
    block = 1024
    steps = width // block
    part = width // 8

    def body(place_ref, x_ref, q_ref, wg_ref, wu_ref, hidden_ref, for_gate_ref, for_up_ref, down_ref):
        k = pl.program_id(0)

        @pl.when(k == 0)
        def _():
            for_up_ref[...] = dot_nn(x_ref[...], wg_ref[...])
            for_gate_ref[...] = dot_nn(x_ref[...], wu_ref[...])

        @pl.when((k > 0) & (k < steps - 1))
        def _():
            for_up_ref[...] += dot_nn(x_ref[...], wg_ref[...])
            for_gate_ref[...] += dot_nn(x_ref[...], wu_ref[...])

        @pl.when(k == steps - 1)
        def _():
            gate = for_up_ref[...] + dot_nn(x_ref[...], wg_ref[...])
            up = for_gate_ref[...] + dot_nn(x_ref[...], wu_ref[...])
            sig = jax.nn.sigmoid(gate)
            act = gate * sig
            hidden_ref[...] = (act * up).astype(jnp.bfloat16)
            for_gate_ref[...] = up * sig * (1.0 + gate * (1.0 - sig))
            for_up_ref[...] = act

        @pl.when(k >= steps)
        def _():
            down_ref[...] = dot_tn(hidden_ref[...], q_ref[...]).astype(jnp.bfloat16)

    def column(k, at):
        z, core = at[0] // 2, at[0] % 2
        j = jnp.maximum(k - steps, 0)
        return (0, width // part + (z + 6 - j) % 4 * 2 + 1 - core)

    held = lambda k: jnp.minimum(k, steps - 1)
    out = pl.BlockSpec((rows, units), lambda k, at: (0, 0))
    weight = pl.BlockSpec((None, block, units), lambda k, at: (0, held(k), 0))
    return pl.pallas_call(
        body,
        grid_spec=pltpu.PrefetchScalarGridSpec(
            num_scalar_prefetch=1,
            grid=(steps + 4,),
            in_specs=[
                pl.BlockSpec((rows, block), lambda k, at: (0, held(k))),
                pl.BlockSpec((rows, part), column),
                weight,
                weight,
            ],
            out_specs=[
                out,
                out,
                out,
                pl.BlockSpec((None, units, part), lambda k, at: (jnp.maximum(k - steps, 0), 0, 0)),
            ],
        ),
        out_shape=[
            jax.ShapeDtypeStruct((rows, units), jnp.bfloat16),
            jax.ShapeDtypeStruct((rows, units), jnp.float32),
            jax.ShapeDtypeStruct((rows, units), jnp.float32),
            jax.ShapeDtypeStruct((4, units, part), jnp.bfloat16),
        ],
        compiler_params=params(26),
        cost_estimate=takes(10),
        name="forward",
    )(place, in_hbm(first), in_hbm(first), in_vmem(w_gate), in_vmem(w_up))


def hidden_grad(buf, offset, w_down, for_gate, for_up, after=(), micros=LONG):
    rows = buf.shape[0]
    units, width = w_down.shape[1:]
    block = 1024
    steps = width // block

    def body(q_ref, wd_ref, for_gate_ref, for_up_ref, d_gate_ref, d_up_ref, sum_ref):
        k = pl.program_id(0)
        part = dot_nt(q_ref[...], wd_ref[...])

        @pl.when(k == 0)
        def _():
            sum_ref[...] = part

        @pl.when((k > 0) & (k < steps - 1))
        def _():
            sum_ref[...] += part

        @pl.when(k == steps - 1)
        def _():
            total = sum_ref[...] + part
            d_gate_ref[...] = (total * for_gate_ref[...]).astype(jnp.bfloat16)
            d_up_ref[...] = (total * for_up_ref[...]).astype(jnp.bfloat16)

    tile = pl.BlockSpec((rows, units), lambda k: (0, 0))
    return pl.pallas_call(
        ordered(body, 4, len(after)),
        grid=(steps,),
        in_specs=[
            pl.BlockSpec((rows, block), lambda k: (0, offset * steps + k)),
            pl.BlockSpec((None, units, block), lambda k: (0, 0, k)),
            tile,
            tile,
        ]
        + [ANY] * len(after),
        out_specs=[tile] * 2,
        out_shape=[jax.ShapeDtypeStruct((rows, units), jnp.bfloat16)] * 2,
        scratch_shapes=[pltpu.VMEM((rows, units), jnp.float32)],
        compiler_params=params(24),
        cost_estimate=takes(micros),
        name="hidden_grad",
    )(in_hbm(buf), in_vmem(w_down), for_gate, for_up, *after)


def weight_part(kind, buf, base, width, other, place, own, received=None, after=(), micros=LONG, stay=2):
    rows = buf.shape[0]
    units = other.shape[1]
    shape = (width, units) if kind == "rows" else (units, width)
    half = shape[0] // 2

    def product(buf_ref, other_ref):
        if kind == "rows":
            return dot_tn(buf_ref[...], other_ref[...])
        return dot_tn(other_ref[...], buf_ref[...])

    def plain(place_ref, buf_ref, other_ref, out_ref):
        out_ref[...] = product(buf_ref, other_ref).astype(jnp.bfloat16)

    def summed(place_ref, buf_ref, other_ref, in_ref, fwd_ref, bwd_ref, keep1_ref, keep3_ref, own_ref):
        j = pl.program_id(0)
        total = product(buf_ref, other_ref) + in_ref[...].astype(jnp.float32)
        total = total.astype(jnp.bfloat16)
        low, high = total[:half], total[half:]

        @pl.when(j == 0)
        def _():
            fwd_ref[...] = low
            bwd_ref[...] = high

        @pl.when(j == 1)
        def _():
            keep1_ref[...] = low
            fwd_ref[...] = high

        @pl.when(j == 2)
        def _():
            own_ref[...] = total

        @pl.when(j == 3)
        def _():
            bwd_ref[...] = low
            keep3_ref[...] = high

    def column(j, at):
        z, core = at[0] // 2, at[0] % 2
        wanted = core if own else 1 - core
        return (0, base + (z + 6 - j) % 4 * 2 + wanted)

    ins = [
        pl.BlockSpec((rows, width), column),
        pl.BlockSpec((rows, units), lambda j, at: (0, 0)),
    ]
    flat = jnp.bfloat16
    if received is None:
        outs = pl.BlockSpec((None,) + shape, lambda j, at: (j, 0, 0))
        out_shape = jax.ShapeDtypeStruct((4,) + shape, flat)
        args = (in_hbm(buf), other)
    else:
        ins.append(pl.BlockSpec((None,) + shape, lambda j, at: (j, 0, 0)))
        shapes = [(2, half, shape[1])] * 2 + [(half, shape[1])] * 2 + [shape]
        outs = [pl.BlockSpec(s, lambda j, at, n=len(s): (0,) * n) for s in shapes]
        pair = (None,) + shapes[0][1:]
        outs[0] = pl.BlockSpec(pair, lambda j, at: (jnp.minimum(j, 1), 0, 0))
        outs[1] = pl.BlockSpec(pair, lambda j, at: (j // 3, 0, 0))
        out_shape = [jax.ShapeDtypeStruct(s, flat) for s in shapes[:stay]]
        out_shape += [pltpu.HBM(s, flat) for s in shapes[stay:]]
        args = (in_hbm(buf), other, received)
    ins += [ANY] * len(after)
    body = plain if received is None else summed
    return pl.pallas_call(
        ordered(body, 1 + len(args), len(after)),
        grid_spec=pltpu.PrefetchScalarGridSpec(
            num_scalar_prefetch=1, grid=(4,), in_specs=ins, out_specs=outs
        ),
        out_shape=out_shape,
        compiler_params=params(18),
        cost_estimate=takes(micros),
        name="weight_part",
    )(place, *args, *after)


def input_rows(d_gate, d_up, w_gate, w_up, after=(), micros=LONG):
    rows, units = d_gate.shape
    width = w_gate.shape[1]
    block = 1024

    def body(dg_ref, du_ref, wg_ref, wu_ref, out_ref):
        total = dot_nt(dg_ref[...], wg_ref[...]) + dot_nt(du_ref[...], wu_ref[...])
        out_ref[...] = total.astype(jnp.bfloat16)

    whole = pl.BlockSpec((rows, units), lambda j: (0, 0))
    weight = pl.BlockSpec((None, block, units), lambda j: (0, j, 0))
    return pl.pallas_call(
        ordered(body, 4, len(after)),
        grid=(width // block,),
        in_specs=[whole, whole, weight, weight] + [ANY] * len(after),
        out_specs=pl.BlockSpec((rows, block), lambda j: (0, j)),
        out_shape=pltpu.HBM((rows, width), jnp.bfloat16),
        compiler_params=params(24),
        cost_estimate=takes(micros),
        name="input_rows",
    )(d_gate, d_up, in_vmem(w_gate), in_vmem(w_up), *after)


def passed_on(parts, hop, after=(), micros=LONG, where=in_hbm):
    half, width = parts[2].shape

    def body(up_ref, down_ref, low_ref, high_ref, fwd_ref, bwd_ref):
        fwd = up_ref[...].astype(jnp.float32) + low_ref[...].astype(jnp.float32)
        bwd = down_ref[...].astype(jnp.float32) + high_ref[...].astype(jnp.float32)
        fwd_ref[...] = fwd.astype(jnp.bfloat16)
        bwd_ref[...] = bwd.astype(jnp.bfloat16)

    block = half // 2
    flat = pl.BlockSpec((block, width), lambda j: (j, 0))
    first = pl.BlockSpec((None, block, width), lambda j: (0, j, 0))
    return pl.pallas_call(
        ordered(body, 4, len(after)),
        grid=(2,),
        in_specs=[flat, flat, first, first] + [ANY] * len(after),
        out_specs=[flat, flat],
        out_shape=[jax.ShapeDtypeStruct((half, width), jnp.bfloat16)] * 2,
        compiler_params=params(8),
        cost_estimate=takes(micros),
        name="passed_on",
    )(where(parts[2]), where(parts[3]), *hop, *after)


def finished(parts, hop, last, after=(), micros=LONG):
    half, width = parts[2].shape

    def body(own_ref, ahead_ref, behind_ref, low_ref, high_ref, out_ref):
        own = own_ref[...].astype(jnp.float32)

        def store(near_ref, far_ref):
            total = own + near_ref[...].astype(jnp.float32) + far_ref[...].astype(jnp.float32)
            out_ref[...] = (total * weight_factor).astype(jnp.bfloat16)

        @pl.when(pl.program_id(0) == 0)
        def _():
            store(ahead_ref, low_ref)

        @pl.when(pl.program_id(0) == 1)
        def _():
            store(behind_ref, high_ref)

    tile = pl.BlockSpec((half, width), lambda j: (j, 0))
    second = pl.BlockSpec((None, half, width), lambda j: (1, 0, 0))
    whole = pl.BlockSpec((half, width), lambda j: (0, 0))
    return pl.pallas_call(
        ordered(body, 5, len(after)),
        grid=(2,),
        in_specs=[tile, second, second, whole, whole] + [ANY] * len(after),
        out_specs=tile,
        out_shape=jax.ShapeDtypeStruct((2 * half, width), jnp.bfloat16),
        compiler_params=params(10),
        cost_estimate=takes(micros),
        name="finished",
    )(in_hbm(parts[4]), hop[1], hop[0], *last, *after)


def combine(select, returned, after=()):
    slots, tok = select.shape
    width = returned.shape[1]
    block = 2048

    def body(sel_ref, in_ref, out_ref):
        out_ref[...] = dot_tn(sel_ref[...], in_ref[...]).astype(jnp.bfloat16)

    return pl.pallas_call(
        ordered(body, 2, len(after)),
        grid=(width // block,),
        in_specs=[
            pl.BlockSpec((slots, tok), lambda j: (0, 0)),
            pl.BlockSpec((slots, block), lambda j: (0, j)),
        ]
        + [ANY] * len(after),
        out_specs=pl.BlockSpec((tok, block), lambda j: (0, j)),
        out_shape=jax.ShapeDtypeStruct((tok, width), jnp.bfloat16),
        compiler_params=params(16),
        cost_estimate=takes(5),
        name="combine",
    )(in_hbm(select), in_hbm(returned), *after)


def shards(tokens_in, out_grad, expert_ids, router_codes, amax_history, w_gate, w_up, w_down):
    n_dp = lax.axis_size("dp")
    peers = lax.axis_size("expert")
    width = tokens_in.shape[1]
    experts = amax_history.shape[0]
    part = width // n_dp
    place = lax.axis_index("dp").astype(jnp.int32).reshape(1)

    swap = [(i, i ^ 1) for i in range(n_dp)]
    ahead = [(i, (i + 2) % n_dp) for i in range(n_dp)]
    behind = [(i, (i - 2) % n_dp) for i in range(n_dp)]

    def exchange(buf):
        blocks = buf.reshape(peers, -1, buf.shape[1])
        out = lax.all_to_all(blocks, "expert", split_axis=0, concat_axis=0, tiled=True)
        return out.reshape(buf.shape)

    def named(parts):
        return (*parts[:2], *[in_hbm(value) for value in parts[2:]])

    def swapped(value):
        return lax.ppermute(value, "dp", swap)

    def one_hop(fwd, bwd):
        return lax.ppermute(fwd, "dp", ahead), lax.ppermute(bwd, "dp", behind)

    sent, select = pack(
        tokens_in, out_grad, expert_ids.T, router_codes.T, amax_history.T, place
    )
    rows = exchange(sent)
    hidden, for_gate, for_up, other_down = forward(rows, w_gate, w_up, place)
    down = ("columns", rows, width // part, part, hidden)
    d_gate, d_up = hidden_grad(rows, 1, w_down, for_gate, for_up, after=(other_down,), micros=MICROS['hg'])
    own_down = weight_part(*down, place, True, swapped(other_down), after=(d_gate,), micros=MICROS['wD'])
    hop_down = one_hop(*own_down[:2])
    gate = ("rows", rows, 0, part, d_gate)
    other_gate = weight_part(
        *gate, place, False, after=named(own_down), micros=MICROS["oG"]
    )
    rows_back = input_rows(
        d_gate, d_up, w_gate, w_up, after=(other_gate,), micros=MICROS["i0"]
    )
    back = exchange(rows_back)
    next_down = passed_on(
        own_down, hop_down, after=(in_hbm(rows_back),), micros=MICROS["nD"]
    )
    last_down = one_hop(*next_down)
    own_gate = weight_part(
        *gate, place, True, swapped(other_gate), after=next_down, micros=MICROS["wG"]
    )
    up = ("rows", rows, 0, part, d_up)
    other_up = weight_part(*up, place, False, after=named(own_gate), micros=MICROS["oU"])
    hop_gate = one_hop(*own_gate[:2])
    grad_down = finished(own_down, hop_down, last_down, after=(other_up,), micros=MICROS["fD"])
    own_up = weight_part(
        *up, place, True, swapped(other_up), after=(in_hbm(grad_down),), micros=MICROS["wU"], stay=4
    )
    hop_up = one_hop(*own_up[:2])
    next_gate = passed_on(own_gate, hop_gate, after=own_up[:2], micros=MICROS["nG"])
    last_gate = one_hop(*next_gate)
    next_up = passed_on(
        own_up, hop_up, after=next_gate, micros=MICROS["nU"], where=lambda value: value
    )
    last_up = one_hop(*next_up)
    grad_tokens = combine(select, back, after=next_up)
    grad_gate = finished(own_gate, hop_gate, last_gate, after=(in_hbm(grad_tokens),), micros=MICROS["fG"])
    grad_up = finished(own_up, hop_up, last_up, after=(in_hbm(grad_gate),), micros=MICROS["fU"])
    return (grad_tokens, grad_gate[None], grad_up[None], grad_down[None])


def solution(mesh):
    return jax.shard_map(
        shards,
        mesh=mesh,
        in_specs=(
            P(("dp", "expert"), None),
            P(("dp", "expert"), None),
            P(("dp", "expert"), None),
            P(("dp", "expert"), None),
            P(),
            P("expert", None, None),
            P("expert", None, None),
            P("expert", None, None),
        ),
        out_specs=(
            P(("dp", "expert"), None),
            P("expert", "dp", None),
            P("expert", "dp", None),
            P("expert", None, "dp"),
        ),
        check_vma=False,
    )
```
